768 devices in a mesh: dp: 96 (over y, x, z_hi), head: 8 (over z_lo, core).
Axes of the slice: x: 4, y: 8, z: 12 (z_hi: 3, z_lo: 4; z = z_hi * 4 + z_lo), core: 2. Of those that a mesh axis runs over, the one named last changes fastest.
Arguments:
- tokens: bfloat16 [24576, 2048], P('dp'), may hold values from -6 to 6
- weights: bfloat16 [8, 768, 2048], P('head', 'dp'), may hold values from -0.13479223 to 0.13479223, as said below
- query_gain: float32 [128], replicated, may hold values from 0.25 to 1.75
- key_gain: float32 [128], replicated, may hold values from 0.25 to 1.75
- first_row: int32 [24576], P('dp'), may hold values from 0 to 24575, as said below
- cotangent: bfloat16 [24576, 4096], P('dp', 'head'), may hold values from -6 to 6
Outputs:
- attended: bfloat16 [24576, 4096], P('dp', 'head')
- token_grad: bfloat16 [24576, 2048], P('dp', 'head')
- weight_grad: float32 [8, 768, 2048], P('head', 'dp')
The draws below stay inside these ranges and needn't reach their ends.
Inputs may be any that keep to these rules, and one draw needn't show every extreme that they name: first_row[i] is the position of the first row of row i's document: documents are runs of consecutive rows, each at most 512 rows long, one of exactly 512 rows, and the last row begins a document of its own. For every even g, weights[g] and weights[g + 1] are equal in their last 256 rows: each key-value head is held by two head devices.
All inputs are finite; a program needn't handle non-finite values.
Results may differ from the reference program's by a relative error of at most 0.017.
Values may be sent and summed in bfloat16 or wider, within the bound.
A program may use at most 32 MiB of HBM per device.

```python
import math
import jax
import jax.numpy as jnp
from jax import lax

D = 2048
HD = 128
QH_DEV = 4
QHEADS = 32
COLS = 768
ROWS = 256
SPAN = 2
MOST = 512
TOKENS = 24576
N_HEAD = 8


def draw_weights(key, part):
    base = jax.random.normal(jax.random.fold_in(key, 11), (N_HEAD, COLS, D), jnp.float32)
    base = jnp.clip(base, -6.0, 6.0) * (1.0 / D ** 0.5)
    split_row = QH_DEV * HD
    shared = jnp.repeat(base[0::2, split_row:], 2, axis=0)
    return jnp.concatenate([base[:, :split_row], shared], axis=1).astype(jnp.bfloat16)


def draw_first_row(key, part):
    total_rows = TOKENS
    blocks = total_rows // ROWS
    key_period, key_marks, key_place = jax.random.split(jax.random.fold_in(key, 7), 3)
    period = jax.random.randint(key_period, (blocks,), 4, 2 * MOST + 1)
    period_rows = jnp.repeat(period, ROWS)
    random_marks = jax.random.randint(key_marks, (total_rows,), 0, 1048576)
    boundary = random_marks % period_rows == 0
    place_start = jax.random.randint(key_place, (), 0, total_rows - MOST)
    position = jnp.arange(total_rows, dtype=jnp.int32)
    inside = (position > place_start) & (position < place_start + MOST)
    boundary = jnp.where(inside, False, boundary)
    boundary = boundary | (position == place_start) | (position == place_start + MOST) | (position == 0) | (position == total_rows - 1)

    def advance(current, item):
        row_index, row_mark = item
        fresh = row_mark | (row_index - current >= MOST)
        current = jnp.where(fresh, row_index, current)
        return (current, current)
    last_start, starts = lax.scan(advance, jnp.int32(0), (position, boundary))
    return starts.astype(jnp.int32)


def level_of(key, dims, cuts, smallest, largest):
    level = 1.0
    for dim, shards_of in cuts:
        draws = jax.random.uniform(jax.random.fold_in(jax.random.fold_in(key, 6), dim), (shards_of,), jnp.float32, smallest / len(cuts), largest / len(cuts))
        level = level * jnp.repeat(jnp.exp(draws), dims[dim] // shards_of).reshape((-1,) + (1,) * (len(dims) - 1 - dim))
    return level


def normal_values(key, dims, spread, reach, cuts=(), kind=jnp.bfloat16):
    drawn = spread * jax.random.normal(key, dims, jnp.float32)
    if cuts:
        drawn = drawn * level_of(key, dims, cuts, -0.22, 0.18)
    return jnp.clip(drawn, -reach, reach).astype(kind)


def setup_inputs(seed: int = 0) -> dict:
    seeds = jax.random.split(jax.random.key(seed), 7)
    tokens = normal_values(seeds[0], (TOKENS, D), 1.0, 6.0, ((0, 96),))
    weights = draw_weights(jax.random.fold_in(seeds[6], 71), 0)
    query_gain = jnp.clip(1.0 + 0.15 * jax.random.normal(seeds[2], (HD,), jnp.float32), 0.25, 1.75)
    key_gain = jnp.clip(1.0 + 0.15 * jax.random.normal(seeds[3], (HD,), jnp.float32), 0.25, 1.75)
    first_row = draw_first_row(jax.random.fold_in(seeds[6], 71), 0)
    cotangent = normal_values(seeds[5], (TOKENS, QHEADS * HD), 1.0, 6.0, ((0, 96), (1, 8)))
    return {"tokens": tokens, "weights": weights, "query_gain": query_gain, "key_gain": key_gain, "first_row": first_row, "cotangent": cotangent}


EPSILON = 1e-06
THETA = 1000000.0
STRETCH = 0.25

def rounded(values):
    return lax.optimization_barrier(values.astype(jnp.bfloat16)).astype(jnp.float32)

def rope_tables(position, head_size):
    middle = head_size // 2
    channel = jnp.arange(middle, dtype=jnp.float32)
    frequency = THETA ** (-2.0 * channel / head_size)
    angles = (position.astype(jnp.float32) * STRETCH)[:, None] * frequency[None, :]
    angles = jnp.concatenate([angles, angles], axis=1)
    return (jnp.cos(angles), jnp.sin(angles))

def normalize_rotate(values, scaling, cosine_table, sine_table):
    factor = lax.rsqrt(lax.optimization_barrier(jnp.mean(values * values, axis=-1, keepdims=True)) + EPSILON)
    normed = values * factor * scaling
    middle = normed.shape[-1] // 2
    turned = jnp.concatenate([-normed[..., middle:], normed[..., :middle]], axis=-1)
    return normed * cosine_table + turned * sine_table

def prepare(projected, query_gain, key_gain, cosine_table, sine_table):
    head_size = query_gain.shape[0]
    head_count = projected.shape[1] // head_size - 2
    row_count = projected.shape[0]
    queries = projected[:, :head_count * head_size].reshape(row_count, head_count, head_size)
    queries = normalize_rotate(queries, query_gain, cosine_table[:, None, :], sine_table[:, None, :])
    key_part = normalize_rotate(projected[:, head_count * head_size:(head_count + 1) * head_size], key_gain, cosine_table, sine_table)
    value_part = projected[:, (head_count + 1) * head_size:]
    return (queries, key_part, value_part)

def attend_block(queries, key_window, value_window, upstream, first_rows, query_place, key_place):
    head_size = queries.shape[-1]
    score_scale = 1.0 / math.sqrt(head_size)
    visible = (key_place[None, :] >= first_rows[:, None]) & (key_place[None, :] <= query_place[:, None])
    score = jnp.einsum('rhc,kc->rhk', queries.astype(jnp.float32), key_window.astype(jnp.float32)) * score_scale
    weight = jnp.where(visible[:, None, :], jnp.exp(score), 0.0)
    denominator = lax.optimization_barrier(jnp.sum(weight, axis=-1))
    summed = jnp.einsum('rhk,kc->rhc', rounded(weight), value_window.astype(jnp.float32))
    attended = (summed / denominator[..., None]).astype(jnp.bfloat16)
    probability = weight / denominator[..., None]
    upstream_float = upstream.astype(jnp.float32)
    row_delta = lax.optimization_barrier(jnp.sum(upstream_float * attended.astype(jnp.float32), axis=-1))
    grad_prob = jnp.einsum('rhc,kc->rhk', upstream_float, value_window.astype(jnp.float32))
    grad_score = rounded(probability * (grad_prob - row_delta[..., None]) * score_scale)
    grad_query = jnp.einsum('rhk,kc->rhc', grad_score, key_window.astype(jnp.float32))
    grad_key = jnp.einsum('rhk,rhc->kc', grad_score, queries.astype(jnp.float32))
    grad_value = jnp.einsum('rhk,rhc->kc', rounded(probability), upstream_float)
    return (attended, grad_query, grad_key, grad_value)

def reference(tokens, weights, query_gain, key_gain, first_row, cotangent):
    total_rows = tokens.shape[0]
    groups = weights.shape[0]
    head_size = query_gain.shape[0]
    head_count = weights.shape[1] // head_size - 2
    blocks = total_rows // ROWS
    reach_rows = SPAN * ROWS
    window = (SPAN + 1) * ROWS
    position = jnp.arange(total_rows, dtype=jnp.int32)
    cosine_table, sine_table = rope_tables(position, head_size)
    padded_place = jnp.arange(total_rows + reach_rows, dtype=jnp.int32) - reach_rows
    outputs = []
    weight_grads = []
    token_grad = jnp.zeros((total_rows, tokens.shape[1]), jnp.float32)
    for group_index in range(groups):
        projected = jnp.dot(tokens, weights[group_index].T, preferred_element_type=jnp.float32)
        prepared, pullback = jax.vjp(lambda values: prepare(values, query_gain, key_gain, cosine_table, sine_table), projected)
        queries = prepared[0].astype(jnp.bfloat16)
        key_value = jnp.concatenate([prepared[1], prepared[2]], axis=1).astype(jnp.bfloat16)
        padded = jnp.concatenate([jnp.zeros((reach_rows, 2 * head_size), jnp.bfloat16), key_value], axis=0)
        width_begin = group_index * head_count * head_size
        upstream = cotangent[:, width_begin:width_begin + head_count * head_size].reshape(total_rows, head_count, head_size)

        def one_block(block_index):
            block_begin = (block_index * ROWS).astype(jnp.int32)
            block_query = lax.dynamic_slice_in_dim(queries, block_begin, ROWS, 0)
            block_pairs = lax.dynamic_slice_in_dim(padded, block_begin, window, 0)
            block_keys = lax.dynamic_slice_in_dim(padded_place, block_begin, window, 0)
            block_upstream = lax.dynamic_slice_in_dim(upstream, block_begin, ROWS, 0)
            block_first = lax.dynamic_slice_in_dim(first_row, block_begin, ROWS, 0)
            block_rows = lax.dynamic_slice_in_dim(position, block_begin, ROWS, 0)
            return attend_block(block_query, block_pairs[:, :head_size], block_pairs[:, head_size:], block_upstream, block_first, block_rows, block_keys)
        attended, grad_query, grad_key, grad_value = lax.map(one_block, jnp.arange(blocks, dtype=jnp.int32))
        slot_grads = jnp.concatenate([grad_key, grad_value], axis=-1).reshape(blocks, SPAN + 1, ROWS, 2 * head_size)
        collected = jnp.zeros((blocks + SPAN, ROWS, 2 * head_size), jnp.float32)
        for offset in range(SPAN + 1):
            collected = collected + jnp.pad(slot_grads[:, offset], ((offset, SPAN - offset), (0, 0), (0, 0)))
        pair_grad = collected[SPAN:].reshape(total_rows, 2 * head_size)
        grad_projected = pullback((grad_query.reshape(total_rows, head_count, head_size), pair_grad[:, :head_size], pair_grad[:, head_size:]))[0]
        grad_projected = grad_projected.astype(jnp.bfloat16)
        token_grad = token_grad + rounded(jnp.dot(grad_projected, weights[group_index], preferred_element_type=jnp.float32))
        weight_grads.append(jnp.dot(grad_projected.T, tokens, preferred_element_type=jnp.float32))
        outputs.append(attended.reshape(total_rows, head_count * head_size))
    stacked = jnp.stack(weight_grads)
    split_row = head_count * head_size
    partner = stacked.reshape(groups // 2, 2, stacked.shape[1], stacked.shape[2])[:, ::-1].reshape(stacked.shape)
    shared_sum = stacked[:, split_row:] + partner[:, split_row:]
    weight_grad = jnp.concatenate([stacked[:, :split_row], shared_sum], axis=1)
    return (jnp.concatenate(outputs, axis=1), token_grad.astype(jnp.bfloat16), weight_grad)
```

```python
import math

import jax
import jax.numpy as jnp
from jax import lax
from jax.experimental import pallas as pl
from jax.experimental.pallas import tpu as pltpu
from jax.sharding import PartitionSpec as P

HD = 128
QH_DEV = 4
COLS = 768
ROWS = 256
SPAN = 2


EPSILON = 1e-06
THETA = 1000000.0
STRETCH = 0.25


NY, NX, NZ = 8, 4, 3
D = 2048
CA = 896
CB = D - CA
CH = CB // 256 * 128
MESH = pl.DeviceIdType.MESH
BF, F32 = jnp.bfloat16, jnp.float32


class Links:
    def __init__(self, send_sem, recv_sem):
        self.send_sem, self.recv_sem = send_sem, recv_sem
        self.sent = []

    def send(self, src, dst, target):
        n = len(self.sent)
        copy = pltpu.make_async_remote_copy(
            src_ref=src, dst_ref=dst, send_sem=self.send_sem.at[n], recv_sem=self.recv_sem.at[n],
            device_id=target, device_id_type=MESH)
        copy.start()
        self.sent.append(copy)
        return copy

    def finish(self):
        for copy in self.sent:
            copy.wait_send()


def rounds(sequences):
    live = list(sequences)
    while live:
        still = []
        for s in live:
            if next(s, 0) is None:
                still.append(s)
        live = still
        yield


def places():
    dp, head = lax.axis_index("dp"), lax.axis_index("head")
    return dp // (NX * NZ), (dp // NZ) % NX, dp % NZ, head


def at(y, x, z, head):
    return (((y + NY) % NY * NX + (x + NX) % NX) * NZ + (z + NZ) % NZ, head)


def ry(y):
    return (y + NY) % NY


def rx(x):
    return (x + NX) % NX


def rz(z):
    return (z + NZ) % NZ


def peers(y, x, z, head):
    out = [at(y + 1, x, z, head), at(y - 1, x, z, head)]
    out += [at(y, x + d, z, head) for d in (1, 2, 3)]
    out += [at(y, x, z + d, head) for d in (1, 2)]
    return out


def enter(targets):
    barrier = pltpu.get_barrier_semaphore()
    for t in targets:
        pl.semaphore_signal(barrier, inc=1, device_id=t, device_id_type=MESH)
    pl.semaphore_wait(barrier, len(targets))


A = pl.ds(0, CA)
B = pl.ds(CA, CB)


def gather_rows(links, w, y, x, z, head):
    up, down = at(y + 1, x, z, head), at(y - 1, x, z, head)
    right, left, across = (at(y, x + d, z, head) for d in (1, -1, 2))
    own = w.at[y, x, z]
    far = [links.send(own, own, at(y, x, z + d, head)) for d in (1, 2)]

    def seq_a(k):
        r = w.at[y, x, k, :, A]
        s = [links.send(r, r, t) for t in (right, left, across)]
        yield
        for step in range(4):
            for c in s:
                c.wait_recv()
            s = []
            for sign, t, half in ((-1, up, 0), (1, down, NX // 2)):
                xs = pl.ds(0, NX) if step < 3 else pl.ds(half, NX // 2)
                r = w.at[ry(y + sign * step), xs, k, :, A]
                s.append(links.send(r, r, t))
            yield
        for c in s:
            c.wait_recv()

    def seq_b(k):
        s = []
        for step in range(4):
            for c in s:
                c.wait_recv()
            s = []
            for sign, t, half in ((-1, up, pl.ds(CA, CH)), (1, down, pl.ds(CA + CH, CB - CH))):
                r = w.at[ry(y + sign * step), x, k, :, B if step < 3 else half]
                s.append(links.send(r, r, t))
            yield
        for c in s:
            c.wait_recv()
        r = w.at[:, x, k, :, B]
        s = [links.send(r, r, t) for t in (right, left)]
        yield
        for c in s:
            c.wait_recv()
        s = []
        for d, t, h in ((-1, right, 0), (1, left, NY // 2)):
            r = w.at[pl.ds(h, NY // 2), rx(x + d), k, :, B]
            s.append(links.send(r, r, t))
        yield
        for c in s:
            c.wait_recv()

    def seq(d):
        if d:
            yield
            far[d - 1].wait_recv()
        k = rz(z - d)
        yield from rounds([seq_b(k), seq_a(k)])

    yield from rounds([seq(0), seq(1), seq(2)])


N_GATHER = 2 + 3 * (3 + 8 + 8 + 4)
N_SCATTER = 2 + 3 * (3 + 8 + 8 + 4) + 1
SCATTER_LANDING = [
    pltpu.VMEM((NZ, 2, 4, NX, 8, CA), BF),
    pltpu.VMEM((NZ, 3, 8, CA), BF),
    pltpu.VMEM((NZ, 2, NY // 2, 8, CB), BF),
    pltpu.VMEM((NZ, 2, NY, 8, CB), BF),
    pltpu.VMEM((NZ, 2, 4, 8, CB), BF),
    pltpu.VMEM((2, 8, D), BF),
]


def scatter_rows(links, g, landing, y, x, z, head):
    lay, lax_, lbx1, lbx2, lby, lz = landing
    up, down = at(y + 1, x, z, head), at(y - 1, x, z, head)
    right, left, across = (at(y, x + d, z, head) for d in (1, -1, 2))

    def add(here, *theirs):
        total = g[here].astype(F32)
        for ref, idx in theirs:
            total = total + ref[idx].astype(F32)
        g[here] = total.astype(BF)

    rows = slice(None)

    def seq_a(k):
        s = []
        for step in range(4):
            n = []
            for i, (sign, t) in enumerate(((1, up), (-1, down))):
                slab = ry(y + sign * (4 - step))
                half = pl.ds(i * (NX // 2), NX // 2)
                if step:
                    s[i].wait_recv()
                    xs = half if step == 1 else pl.ds(0, NX)
                    add((slab, xs, k, rows, A), (lay, (k, i, step - 1, xs)))
                xs = half if step == 0 else pl.ds(0, NX)
                n.append(links.send(g.at[slab, xs, k, :, A], lay.at[k, i, step, xs], t))
            s = n
            yield
        for c in s:
            c.wait_recv()
        add((y, pl.ds(0, NX), k, rows, A), (lay, (k, 0, 3)), (lay, (k, 1, 3)))
        s = [links.send(g.at[y, rx(x + d), k, :, A], lax_.at[k, d - 1], t)
             for d, t in ((1, right), (2, across), (3, left))]
        yield
        for c in s:
            c.wait_recv()
        add((y, x, k, rows, A), (lax_, (k, 0)), (lax_, (k, 1)), (lax_, (k, 2)))

    def seq_b(k):
        s = []
        for i, t in enumerate((right, left)):
            ys = pl.ds(i * (NY // 2), NY // 2)
            s.append(links.send(g.at[ys, rx(x + 2), k, :, B], lbx1.at[k, i], t))
        yield
        n = []
        for i, (sign, t) in enumerate(((1, right), (-1, left))):
            ys = pl.ds(i * (NY // 2), NY // 2)
            s[i].wait_recv()
            add((ys, rx(x + sign), k, rows, B), (lbx1, (k, i)))
            n.append(links.send(g.at[:, rx(x + sign), k, :, B], lbx2.at[k, i], t))
        yield
        for c in n:
            c.wait_recv()
        add((pl.ds(0, NY), x, k, rows, B), (lbx2, (k, 0)), (lbx2, (k, 1)))
        s = []
        halves = (pl.ds(0, CH), pl.ds(CH, CB - CH))
        for step in range(4):
            n = []
            for i, (sign, t) in enumerate(((1, up), (-1, down))):
                slab = ry(y + sign * (4 - step))
                if step:
                    s[i].wait_recv()
                    h = halves[i] if step == 1 else pl.ds(0, CB)
                    add((slab, x, k, rows, pl.ds(CA + h.start, h.size)), (lby, (k, i, step - 1, rows, h)))
                h = pl.ds(0, CB) if step else halves[i]
                n.append(links.send(g.at[slab, x, k, :, pl.ds(CA + h.start, h.size)], lby.at[k, i, step, :, h], t))
            s = n
            yield
        for c in s:
            c.wait_recv()
        add((y, x, k, rows, B), (lby, (k, 0, 3)), (lby, (k, 1, 3)))

    sent = []

    def seq(d):
        k = rz(z + d)
        yield from rounds([seq_b(k), seq_a(k)])
        if d:
            sent.append(links.send(g.at[y, x, k], lz.at[d - 1], at(y, x, k, head)))

    yield from rounds([seq(1), seq(2), seq(0)])
    for c in sent:
        c.wait_recv()
    yield


WHOLE = pl.BlockSpec(memory_space=pltpu.VMEM)
BLOCKS = (NY, NX, NZ, 8, D)


def gather_kernel(w_ref, o_ref, w, send_sem, recv_sem):
    y, x, z, head = places()
    w[y, x, z] = w_ref[0]
    enter(peers(y, x, z, head))
    links = Links(send_sem, recv_sem)
    for _ in gather_rows(links, w, y, x, z, head):
        pass
    links.finish()
    o_ref[...] = w[...]


def gather_weights(w):
    return pl.pallas_call(
        gather_kernel,
        out_shape=jax.ShapeDtypeStruct(BLOCKS, BF),
        in_specs=[WHOLE],
        out_specs=WHOLE,
        scratch_shapes=[
            pltpu.VMEM(BLOCKS, BF),
            pltpu.SemaphoreType.DMA((N_GATHER,)),
            pltpu.SemaphoreType.DMA((N_GATHER,)),
        ],
        compiler_params=pltpu.CompilerParams(
            collective_id=1, has_side_effects=True, vmem_limit_bytes=40 << 20
        ),
        name="gather_weights",
    )(w)


def scatter_kernel(g_ref, o_ref, *scratch):
    g, landing = scratch[0], scratch[1:7]
    pair_out, pair_in, send_sem, recv_sem = scratch[7:]
    y, x, z, head = places()
    dp = lax.axis_index("dp")
    sibling = (dp, head + 1 - 2 * (head % 2))
    enter(peers(y, x, z, head) + [sibling])
    g[...] = g_ref[...]
    links = Links(send_sem, recv_sem)
    for _ in scatter_rows(links, g, landing, y, x, z, head):
        pass
    own = g[y, x, z].astype(F32) + landing[5][0].astype(F32) + landing[5][1].astype(F32)
    pair_out[...] = own.astype(BF)
    links.send(pair_out, pair_in, sibling).wait_recv()
    shared = dp * 8 >= QH_DEV * HD
    o_ref[0] = own + jnp.where(shared, pair_in[...].astype(F32), 0.0)
    links.finish()


def scatter_grads(g):
    return pl.pallas_call(
        scatter_kernel,
        out_shape=jax.ShapeDtypeStruct((1, 8, D), F32),
        in_specs=[WHOLE],
        out_specs=WHOLE,
        scratch_shapes=[
            pltpu.VMEM(BLOCKS, BF),
            *SCATTER_LANDING,
            pltpu.VMEM((8, D), BF),
            pltpu.VMEM((8, D), BF),
            pltpu.SemaphoreType.DMA((N_SCATTER,)),
            pltpu.SemaphoreType.DMA((N_SCATTER,)),
        ],
        compiler_params=pltpu.CompilerParams(
            collective_id=2, has_side_effects=True, vmem_limit_bytes=40 << 20
        ),
        name="scatter_grads",
    )(g)


def from_behind(x, axis, by):
    devices = lax.axis_size(axis)
    pairs = [(i, i + by) for i in range(devices) if 0 <= i + by < devices]
    return lax.ppermute(x, axis, pairs)


def rope_tables(position, head_size):
    middle = head_size // 2
    channel = jnp.arange(middle, dtype=jnp.float32)
    frequency = THETA ** (-2.0 * channel / head_size)
    angles = (position.astype(jnp.float32) * STRETCH)[:, None] * frequency[None, :]
    angles = jnp.concatenate([angles, angles], axis=1)
    return (jnp.cos(angles), jnp.sin(angles))


def normalize_rotate(values, scaling, cosine_table, sine_table):
    factor = lax.rsqrt(jnp.mean(values * values, axis=-1, keepdims=True) + EPSILON)
    normed = values * factor * scaling
    middle = normed.shape[-1] // 2
    turned = jnp.concatenate([-normed[..., middle:], normed[..., :middle]], axis=-1)
    return normed * cosine_table + turned * sine_table


def prepare(projected, query_gain, key_gain, cosine_table, sine_table):
    row_count = projected.shape[0]
    queries = projected[:, : QH_DEV * HD].reshape(row_count, QH_DEV, HD)
    queries = normalize_rotate(
        queries, query_gain, cosine_table[:, None, :], sine_table[:, None, :]
    )
    key_part = normalize_rotate(
        projected[:, QH_DEV * HD : (QH_DEV + 1) * HD], key_gain, cosine_table, sine_table
    )
    value_part = projected[:, (QH_DEV + 1) * HD :]
    return (queries, key_part, value_part)


def attend_window(queries, window, upstream, first_rows, query_place, key_place):
    score_scale = 1.0 / math.sqrt(HD)
    key_window = window[:, :HD]
    value_window = window[:, HD:]
    visible = (key_place[None, :] >= first_rows[:, None]) & (
        key_place[None, :] <= query_place[:, None]
    )
    score = (
        jnp.einsum("rhc,kc->rhk", queries, key_window, preferred_element_type=jnp.float32)
        * score_scale
    )
    weight = jnp.where(visible[:, None, :], jnp.exp(score), 0.0)
    denominator = jnp.sum(weight, axis=-1)
    summed = jnp.einsum(
        "rhk,kc->rhc", weight.astype(jnp.bfloat16), value_window, preferred_element_type=jnp.float32
    )
    attended = (summed / denominator[..., None]).astype(jnp.bfloat16)
    probability = weight / denominator[..., None]
    row_delta = jnp.sum(upstream.astype(jnp.float32) * attended.astype(jnp.float32), axis=-1)
    grad_prob = jnp.einsum(
        "rhc,kc->rhk", upstream, value_window, preferred_element_type=jnp.float32
    )
    grad_score = (probability * (grad_prob - row_delta[..., None]) * score_scale).astype(
        jnp.bfloat16
    )
    grad_query = jnp.einsum(
        "rhk,kc->rhc", grad_score, key_window, preferred_element_type=jnp.float32
    )
    grad_key = jnp.einsum("rhk,rhc->kc", grad_score, queries, preferred_element_type=jnp.float32)
    grad_value = jnp.einsum(
        "rhk,rhc->kc",
        probability.astype(jnp.bfloat16),
        upstream,
        preferred_element_type=jnp.float32,
    )
    return (attended, grad_query, jnp.concatenate([grad_key, grad_value], axis=1))


def body(tokens, weights, query_gain, key_gain, first_row, cotangent):
    block_index = lax.axis_index("dp")
    position = block_index * ROWS + jnp.arange(ROWS, dtype=jnp.int32)
    key_place = (block_index - SPAN) * ROWS + jnp.arange((SPAN + 1) * ROWS, dtype=jnp.int32)
    cosine_table, sine_table = rope_tables(position, HD)
    weight_piece = gather_weights(weights).reshape(1, COLS, D)
    projected = jnp.einsum("rd,cd->rc", tokens, weight_piece[0], preferred_element_type=jnp.float32)
    prepared, pullback = jax.vjp(
        lambda values: prepare(values, query_gain, key_gain, cosine_table, sine_table), projected
    )
    queries = prepared[0].astype(jnp.bfloat16)
    key_value = jnp.concatenate([prepared[1], prepared[2]], axis=1).astype(jnp.bfloat16)
    earlier = [from_behind(key_value, "dp", distance) for distance in range(SPAN, 0, -1)]
    window = jnp.concatenate(earlier + [key_value], axis=0)
    upstream = cotangent.reshape(ROWS, QH_DEV, HD)
    attended, grad_query, slot_grads = attend_window(
        queries, window, upstream, first_row, position, key_place
    )
    pair_grad = slot_grads[SPAN * ROWS :]
    for distance in range(1, SPAN + 1):
        slot_index = SPAN - distance
        pair_grad = pair_grad + from_behind(
            slot_grads[slot_index * ROWS : (slot_index + 1) * ROWS].astype(jnp.bfloat16),
            "dp",
            -distance,
        ).astype(jnp.float32)
    grad_projected = pullback((grad_query, pair_grad[:, :HD], pair_grad[:, HD:]))[0].astype(
        jnp.bfloat16
    )
    partial_grad = jnp.dot(grad_projected, weight_piece[0], preferred_element_type=jnp.float32)
    token_grad = lax.psum_scatter(
        partial_grad.astype(jnp.bfloat16), "head", scatter_dimension=1, tiled=True
    )
    own_grad = jnp.einsum("rc,rd->cd", grad_projected, tokens, preferred_element_type=jnp.float32)
    weight_grad = scatter_grads(own_grad.astype(jnp.bfloat16).reshape(BLOCKS))
    return (attended.reshape(ROWS, QH_DEV * HD), token_grad, weight_grad)


def solution(mesh):
    in_specs = (P("dp", None), P("head", "dp", None), P(), P(), P("dp"), P("dp", "head"))
    out_specs = (P("dp", "head"), P("dp", "head"), P("head", "dp", None))
    return jax.shard_map(body, mesh=mesh, in_specs=in_specs, out_specs=out_specs, check_vma=False)
```

```python
import math

import jax
import jax.numpy as jnp
import numpy as np
from jax import lax
from jax.experimental import pallas as pl
from jax.experimental.pallas import tpu as pltpu
from jax.sharding import PartitionSpec as P

HD = 128
QH_DEV = 4
QC = QH_DEV * HD
COLS = 768
ROWS = 256
SPAN = 2
N_DP = 96
N_LOW = 4
HALF = HD // 2


EPSILON = 1e-06
THETA = 1000000.0
STRETCH = 0.25
SCALE = 1.0 / math.sqrt(HD)


NY, NX, NZ = 8, 4, 3
D = 2048
CA = 896
CB = D - CA
CH = CB // 256 * 128
MESH = pl.DeviceIdType.MESH
BF, F32 = jnp.bfloat16, jnp.float32


class Links:
    def __init__(self, send_sem, recv_sem):
        self.send_sem, self.recv_sem = send_sem, recv_sem
        self.sent = []

    def send(self, src, dst, target):
        n = len(self.sent)
        copy = pltpu.make_async_remote_copy(
            src_ref=src, dst_ref=dst, send_sem=self.send_sem.at[n], recv_sem=self.recv_sem.at[n],
            device_id=target, device_id_type=MESH)
        copy.start()
        self.sent.append(copy)
        return copy

    def finish(self):
        for copy in self.sent:
            copy.wait_send()


def rounds(sequences):
    live = list(sequences)
    while live:
        still = []
        for s in live:
            if next(s, 0) is None:
                still.append(s)
        live = still
        yield


def places():
    dp, head = lax.axis_index("dp"), lax.axis_index("head")
    return dp // (NX * NZ), (dp // NZ) % NX, dp % NZ, head


def at(y, x, z, head):
    return (((y + NY) % NY * NX + (x + NX) % NX) * NZ + (z + NZ) % NZ, head)


def ry(y):
    return (y + NY) % NY


def rx(x):
    return (x + NX) % NX


def rz(z):
    return (z + NZ) % NZ


def peers(y, x, z, head):
    out = [at(y + 1, x, z, head), at(y - 1, x, z, head)]
    out += [at(y, x + d, z, head) for d in (1, 2, 3)]
    out += [at(y, x, z + d, head) for d in (1, 2)]
    return out


def enter(targets):
    barrier = pltpu.get_barrier_semaphore()
    for t in targets:
        pl.semaphore_signal(barrier, inc=1, device_id=t, device_id_type=MESH)
    pl.semaphore_wait(barrier, len(targets))


A = pl.ds(0, CA)
B = pl.ds(CA, CB)


def gather_rows(links, w, y, x, z, head):
    up, down = at(y + 1, x, z, head), at(y - 1, x, z, head)
    right, left, across = (at(y, x + d, z, head) for d in (1, -1, 2))
    own = w.at[y, x, z]
    far = [links.send(own, own, at(y, x, z + d, head)) for d in (1, 2)]

    def seq_a(k):
        r = w.at[y, x, k, :, A]
        s = [links.send(r, r, t) for t in (right, left, across)]
        yield
        for step in range(4):
            for c in s:
                c.wait_recv()
            s = []
            for sign, t, half in ((-1, up, 0), (1, down, NX // 2)):
                xs = pl.ds(0, NX) if step < 3 else pl.ds(half, NX // 2)
                r = w.at[ry(y + sign * step), xs, k, :, A]
                s.append(links.send(r, r, t))
            yield
        for c in s:
            c.wait_recv()

    def seq_b(k):
        s = []
        for step in range(4):
            for c in s:
                c.wait_recv()
            s = []
            for sign, t, half in ((-1, up, pl.ds(CA, CH)), (1, down, pl.ds(CA + CH, CB - CH))):
                r = w.at[ry(y + sign * step), x, k, :, B if step < 3 else half]
                s.append(links.send(r, r, t))
            yield
        for c in s:
            c.wait_recv()
        r = w.at[:, x, k, :, B]
        s = [links.send(r, r, t) for t in (right, left)]
        yield
        for c in s:
            c.wait_recv()
        s = []
        for d, t, h in ((-1, right, 0), (1, left, NY // 2)):
            r = w.at[pl.ds(h, NY // 2), rx(x + d), k, :, B]
            s.append(links.send(r, r, t))
        yield
        for c in s:
            c.wait_recv()

    def seq(d):
        if d:
            yield
            far[d - 1].wait_recv()
        k = rz(z - d)
        yield from rounds([seq_b(k), seq_a(k)])

    yield from rounds([seq(0), seq(1), seq(2)])


N_GATHER = 2 + 3 * (3 + 8 + 8 + 4)
N_SCATTER = 2 + 3 * (3 + 8 + 8 + 4)
SCATTER_LANDING = [
    pltpu.VMEM((NZ, 2, 4, NX, 8, CA), BF),
    pltpu.VMEM((NZ, 3, 8, CA), BF),
    pltpu.VMEM((NZ, 2, NY // 2, 8, CB), BF),
    pltpu.VMEM((NZ, 2, NY, 8, CB), BF),
    pltpu.VMEM((NZ, 2, 4, 8, CB), BF),
    pltpu.VMEM((2, 8, D), BF),
]


def scatter_rows(links, g, landing, y, x, z, head):
    lay, lax_, lbx1, lbx2, lby, lz = landing
    up, down = at(y + 1, x, z, head), at(y - 1, x, z, head)
    right, left, across = (at(y, x + d, z, head) for d in (1, -1, 2))

    def add(here, *theirs):
        total = g[here].astype(F32)
        for ref, idx in theirs:
            total = total + ref[idx].astype(F32)
        g[here] = total.astype(BF)

    rows = slice(None)

    def seq_a(k):
        s = []
        for step in range(4):
            n = []
            for i, (sign, t) in enumerate(((1, up), (-1, down))):
                slab = ry(y + sign * (4 - step))
                half = pl.ds(i * (NX // 2), NX // 2)
                if step:
                    s[i].wait_recv()
                    xs = half if step == 1 else pl.ds(0, NX)
                    add((slab, xs, k, rows, A), (lay, (k, i, step - 1, xs)))
                xs = half if step == 0 else pl.ds(0, NX)
                n.append(links.send(g.at[slab, xs, k, :, A], lay.at[k, i, step, xs], t))
            s = n
            yield
        for c in s:
            c.wait_recv()
        add((y, pl.ds(0, NX), k, rows, A), (lay, (k, 0, 3)), (lay, (k, 1, 3)))
        s = [links.send(g.at[y, rx(x + d), k, :, A], lax_.at[k, d - 1], t)
             for d, t in ((1, right), (2, across), (3, left))]
        yield
        for c in s:
            c.wait_recv()
        add((y, x, k, rows, A), (lax_, (k, 0)), (lax_, (k, 1)), (lax_, (k, 2)))

    def seq_b(k):
        s = []
        for i, t in enumerate((right, left)):
            ys = pl.ds(i * (NY // 2), NY // 2)
            s.append(links.send(g.at[ys, rx(x + 2), k, :, B], lbx1.at[k, i], t))
        yield
        n = []
        for i, (sign, t) in enumerate(((1, right), (-1, left))):
            ys = pl.ds(i * (NY // 2), NY // 2)
            s[i].wait_recv()
            add((ys, rx(x + sign), k, rows, B), (lbx1, (k, i)))
            n.append(links.send(g.at[:, rx(x + sign), k, :, B], lbx2.at[k, i], t))
        yield
        for c in n:
            c.wait_recv()
        add((pl.ds(0, NY), x, k, rows, B), (lbx2, (k, 0)), (lbx2, (k, 1)))
        s = []
        halves = (pl.ds(0, CH), pl.ds(CH, CB - CH))
        for step in range(4):
            n = []
            for i, (sign, t) in enumerate(((1, up), (-1, down))):
                slab = ry(y + sign * (4 - step))
                if step:
                    s[i].wait_recv()
                    h = halves[i] if step == 1 else pl.ds(0, CB)
                    add((slab, x, k, rows, pl.ds(CA + h.start, h.size)), (lby, (k, i, step - 1, rows, h)))
                h = pl.ds(0, CB) if step else halves[i]
                n.append(links.send(g.at[slab, x, k, :, pl.ds(CA + h.start, h.size)], lby.at[k, i, step, :, h], t))
            s = n
            yield
        for c in s:
            c.wait_recv()
        add((y, x, k, rows, B), (lby, (k, 0, 3)), (lby, (k, 1, 3)))

    sent = []

    def seq(d):
        k = rz(z + d)
        yield from rounds([seq_b(k), seq_a(k)])
        if d:
            sent.append(links.send(g.at[y, x, k], lz.at[d - 1], at(y, x, k, head)))

    yield from rounds([seq(1), seq(2), seq(0)])
    for c in sent:
        c.wait_recv()
    yield

WHOLE = pl.BlockSpec(memory_space=pltpu.VMEM)
BLOCKS = (NY, NX, NZ, 8, D)
N_COPIES = N_GATHER + N_SCATTER + 4 + 5 + 7 + 1


def dot(a, b):
    return jnp.dot(a, b, preferred_element_type=F32)


def head_rows(h):
    return pl.ds(pl.multiple_of(h * HD, HD), HD)


def normalize(u, gain):
    factor = lax.rsqrt(jnp.mean(u * u, axis=0, keepdims=True) + EPSILON)
    return u * factor, factor


def rotate(n, cos, sin):
    a, b = n[:HALF], n[HALF:]
    return jnp.concatenate([a * cos - b * sin, b * cos + a * sin], axis=0)


def normalize_rotate_back(u, gain, cos, sin, grad):
    n, factor = normalize(u, gain)
    a, b = grad[:HALF], grad[HALF:]
    back = jnp.concatenate([a * cos + b * sin, b * cos - a * sin], axis=0) * gain
    return factor * (back - n * jnp.mean(back * n, axis=0, keepdims=True))


def layer_kernel(
    tokens,
    w_ref,
    query_gain,
    key_gain,
    frequency,
    first_row,
    cotangent,
    attended,
    token_grad,
    weight_grad,
    w,
    g,
    *scratch,
):
    landing, scratch = scratch[:6], scratch[6:]
    (
        pair_out, pair_in, tokens_t, cot_t, tables, gains, proj_t, q_t, q_n, kv_t, kv_n, weight, denom,
        att_t, dq_t, dkv, d_out, d_pair, d_sum, d_in, gq_t, gq_n, part, tp, tp_pair, tp_low, send_sem, recv_sem,
    ) = scratch
    dp = lax.axis_index("dp")
    y, x, z, head = places()
    low, core = head // 2, head % 2
    other = 1 - core
    sibling = (dp, 2 * low + other)
    ahead = [((dp + d) % N_DP, head) for d in (1, 2)]
    behind = [((dp + N_DP - d) % N_DP, head) for d in (1, 2)]
    lows = [(dp, (low + d) % N_LOW * 2 + core) for d in (1, 2, 3)]
    w[y, x, z] = w_ref[0]
    enter(peers(y, x, z, head) + [sibling] + ahead + behind + lows)
    links = Links(send_sem, recv_sem)
    w2, g2 = w.reshape(COLS, D), g.reshape(COLS, D)

    gather = gather_rows(links, w, y, x, z, head)
    next(gather)
    for c in range(0, D, ROWS):
        tokens_t[pl.ds(c, ROWS)] = tokens[:, pl.ds(c, ROWS)].T
    next(gather)
    cot_t[...] = cotangent[...].T
    square = (HD, HD)
    gains[0] = jnp.broadcast_to(query_gain[...], square).T
    gains[1] = jnp.broadcast_to(key_gain[...], square).T
    rate = jnp.broadcast_to(frequency[...], square).T[:HALF]
    rate = jnp.concatenate([rate, rate], axis=1)
    place = (dp * ROWS + lax.broadcasted_iota(jnp.int32, (HALF, ROWS), 1)).astype(F32)
    angles = place * STRETCH * rate
    tables[0] = jnp.cos(angles)
    tables[1] = jnp.sin(angles)
    for _ in gather:
        pass

    def project(h, _):
        proj_t[head_rows(h)] = dot(w2[head_rows(h)], tokens_t[...])
        return 0

    lax.fori_loop(0, COLS // HD, project, 0)

    def gain_of(i):
        return jnp.concatenate([gains[i], gains[i]], axis=1)

    def prepared(h, i):
        n, _ = normalize(proj_t[head_rows(h)], None)
        return rotate(n * gain_of(i), tables[0], tables[1]).astype(BF)

    kv_t[0, 0] = prepared(QH_DEV, 1)
    kv_t[0, 1] = proj_t[pl.ds(QC + HD, HD)].astype(BF)
    halo = [links.send(kv_t.at[0, core], kv_t.at[d, core], ahead[d - 1]) for d in (1, 2)]

    def natural(j):
        kv_n[j, 0] = kv_t[j, 0].T
        kv_n[j, 1] = kv_t[j, 1].T

    natural(0)

    def prepare_query(h, _):
        turned = prepared(h, 0)
        q_t[head_rows(h)] = turned
        q_n[h] = turned.T
        return 0

    lax.fori_loop(0, QH_DEV, prepare_query, 0)

    row = lax.broadcasted_iota(jnp.int32, (ROWS, ROWS), 1)
    key = lax.broadcasted_iota(jnp.int32, (ROWS, ROWS), 0)

    def forward(j, h):
        key_place = (dp - j) * ROWS + key
        visible = key_place >= first_row[...]
        if j == 0:
            visible = visible & (key <= row)
        score = dot(kv_n[j, 0], q_t[head_rows(h)]) * SCALE
        seen = jnp.where(visible, jnp.exp(score), 0.0)
        weight[h, j] = seen
        return jnp.sum(seen, axis=0, keepdims=True), dot(kv_t[j, 1], seen.astype(BF))

    def own_forward(h, _):
        denom[h], att_t[head_rows(h)] = forward(0, h)
        return 0

    lax.fori_loop(0, QH_DEV, own_forward, 0)

    pair = []
    for d in (1, 2):
        halo[d - 1].wait_recv()
        pair.append(links.send(kv_t.at[d, core], kv_t.at[d, core], sibling))
    for d in (1, 2):
        pair[d - 1].wait_recv()
        natural(d)

    def backward(j, h, inverse, delta):
        probability = weight[h, j] * inverse
        grad_prob = dot(kv_n[j, 1], cot_t[head_rows(h)])
        grad_score = (probability * (grad_prob - delta) * SCALE).astype(BF)
        dk = dot(grad_score, q_n[h])
        dv = dot(probability.astype(BF), cotangent[:, head_rows(h)])
        return dot(kv_t[j, 0], grad_score), dk, dv

    dkv[...] = jnp.zeros_like(dkv)

    def far(h, _):
        total, summed = denom[h], att_t[head_rows(h)]
        for j in (1, 2):
            more, moved = forward(j, h)
            total = total + more
            summed = summed + moved
        inverse = 1.0 / total
        out = (summed * inverse).astype(BF)
        attended[:, head_rows(h)] = out.T
        delta = jnp.sum(cot_t[head_rows(h)].astype(F32) * out.astype(F32), axis=0, keepdims=True)
        denom[h] = inverse
        att_t[head_rows(h)] = jnp.broadcast_to(delta, (HD, ROWS))
        dq = None
        for j in (1, 2):
            more, dk, dv = backward(j, h, inverse, delta)
            dq = more if dq is None else dq + more
            dkv[j, 0] += dk
            dkv[j, 1] += dv
        dq_t[head_rows(h)] = dq
        return 0

    lax.fori_loop(0, QH_DEV, far, 0)

    def to_pair(j):
        d_out[j] = dkv[j, other].astype(BF)
        return links.send(d_out.at[j], d_pair.at[j], sibling)

    back = [to_pair(j) for j in (1, 2)]

    def near(h, _):
        dq, dk, dv = backward(0, h, denom[h], att_t[pl.ds(pl.multiple_of(h * HD, HD), 8)][:1])
        dkv[0, 0] += dk
        dkv[0, 1] += dv
        grad = dq_t[head_rows(h)] + dq
        back_t = normalize_rotate_back(proj_t[head_rows(h)], gain_of(0), tables[0], tables[1], grad).astype(BF)
        gq_t[head_rows(h)] = back_t
        gq_n[:, head_rows(h)] = back_t.T
        return 0

    for j in (1, 2):
        back[j - 1].wait_recv()
        d_sum[j - 1] = (dkv[j, core] + d_pair[j].astype(F32)).astype(BF)
        back[j - 1] = links.send(d_sum.at[j - 1], d_in.at[j - 1], behind[j - 1])
    lax.fori_loop(0, QH_DEV, near, 0)
    back_own = to_pair(0)

    def own_grads(h, _):
        g2[head_rows(h)] = dot(gq_t[head_rows(h)], tokens[...]).astype(BF)
        return 0

    lax.fori_loop(0, QH_DEV, own_grads, 0)
    mine = pl.ds(pl.multiple_of(QC + core * HD, HD), HD)
    theirs = pl.ds(pl.multiple_of(QC + other * HD, HD), HD)
    g2[theirs] = jnp.zeros((HD, D), BF)

    def token_part(i, _):
        cols = pl.ds(pl.multiple_of(i * ROWS, ROWS), ROWS)
        part[i] = dot(gq_n[...], w2[pl.ds(0, QC), cols])
        return 0

    lax.fori_loop(0, 8, token_part, 0)

    back_own.wait_recv()
    total = dkv[0, core] + d_pair[0].astype(F32)
    for j in (0, 1):
        back[j].wait_recv()
        total = total + d_in[j].astype(F32)
    total = total.T
    turned = normalize_rotate_back(proj_t[pl.ds(QC, HD)], gain_of(1), tables[0], tables[1], total)
    total = jnp.where(core == 0, turned, total).astype(BF)
    gk_n = total.T
    g2[mine] = dot(total, tokens[...]).astype(BF)

    scatter = scatter_rows(links, g, landing, y, x, z, head)
    next(scatter)

    def token_rest(i, _):
        cols = pl.ds(pl.multiple_of(i * ROWS, ROWS), ROWS)
        tp[i] = (part[i] + dot(gk_n, w2[mine, cols])).astype(BF)
        return 0

    lax.fori_loop(0, 8, token_rest, 0)
    swap = [links.send(tp.at[2 * i + other], tp_pair.at[i], sibling) for i in range(N_LOW)]
    next(scatter)
    for i in range(N_LOW):
        swap[i].wait_recv()
        tp[2 * i + core] = (tp[2 * i + core].astype(F32) + tp_pair[i].astype(F32)).astype(BF)
    low_copies = [
        links.send(tp.at[(low + d) % N_LOW * 2 + core], tp_low.at[d - 1], lows[d - 1]) for d in (1, 2, 3)
    ]
    for _ in scatter:
        pass
    own = g[y, x, z].astype(F32) + landing[5][0].astype(F32) + landing[5][1].astype(F32)
    pair_out[...] = own.astype(BF)
    last = links.send(pair_out, pair_in, sibling)
    total = tp[head].astype(F32)
    for d in range(3):
        low_copies[d].wait_recv()
        total = total + tp_low[d].astype(F32)
    token_grad[...] = total.astype(BF)
    last.wait_recv()
    weight_grad[0] = own + jnp.where(dp * 8 >= QC, pair_in[...].astype(F32), 0.0)
    links.finish()


def body(tokens, weights, query_gain, key_gain, first_row, cotangent):
    channel = np.arange(HALF, dtype=np.float64)
    rates = (THETA ** (-2.0 * channel / HD)).astype(np.float32)
    frequency = jnp.asarray(np.concatenate([rates, rates])[None])
    return pl.pallas_call(
        layer_kernel,
        out_shape=(
            jax.ShapeDtypeStruct((ROWS, QC), BF),
            jax.ShapeDtypeStruct((ROWS, D // 8), BF),
            jax.ShapeDtypeStruct((1, 8, D), F32),
        ),
        in_specs=[WHOLE] * 7,
        out_specs=[WHOLE] * 3,
        scratch_shapes=[
            pltpu.VMEM(BLOCKS, BF),
            pltpu.VMEM(BLOCKS, BF),
            *SCATTER_LANDING,
            pltpu.VMEM((8, D), BF),
            pltpu.VMEM((8, D), BF),
            pltpu.VMEM((D, ROWS), BF),
            pltpu.VMEM((QC, ROWS), BF),
            pltpu.VMEM((2, HALF, ROWS), F32),
            pltpu.VMEM((2, HD, HD), F32),
            pltpu.VMEM((COLS, ROWS), F32),
            pltpu.VMEM((QC, ROWS), BF),
            pltpu.VMEM((QH_DEV, ROWS, HD), BF),
            pltpu.VMEM((SPAN + 1, 2, HD, ROWS), BF),
            pltpu.VMEM((SPAN + 1, 2, ROWS, HD), BF),
            pltpu.VMEM((QH_DEV, SPAN + 1, ROWS, ROWS), F32),
            pltpu.VMEM((QH_DEV, 1, ROWS), F32),
            pltpu.VMEM((QC, ROWS), F32),
            pltpu.VMEM((QC, ROWS), F32),
            pltpu.VMEM((SPAN + 1, 2, ROWS, HD), F32),
            pltpu.VMEM((SPAN + 1, ROWS, HD), BF),
            pltpu.VMEM((SPAN + 1, ROWS, HD), BF),
            pltpu.VMEM((SPAN, ROWS, HD), BF),
            pltpu.VMEM((SPAN, ROWS, HD), BF),
            pltpu.VMEM((QC, ROWS), BF),
            pltpu.VMEM((ROWS, QC), BF),
            pltpu.VMEM((8, ROWS, ROWS), F32),
            pltpu.VMEM((8, ROWS, ROWS), BF),
            pltpu.VMEM((N_LOW, ROWS, ROWS), BF),
            pltpu.VMEM((N_LOW - 1, ROWS, ROWS), BF),
            pltpu.SemaphoreType.DMA((N_COPIES,)),
            pltpu.SemaphoreType.DMA((N_COPIES,)),
        ],
        compiler_params=pltpu.CompilerParams(
            collective_id=1, has_side_effects=True, vmem_limit_bytes=50 << 20
        ),
        cost_estimate=pl.CostEstimate(flops=4 * 10**9, bytes_accessed=4 << 20, transcendentals=10**6),
        name="masked_attention_layer",
    )(
        tokens,
        weights,
        query_gain.reshape(1, HD),
        key_gain.reshape(1, HD),
        frequency,
        first_row.reshape(1, ROWS),
        cotangent,
    )


def solution(mesh):
    in_specs = (P("dp", None), P("head", "dp", None), P(), P(), P("dp"), P("dp", "head"))
    out_specs = (P("dp", "head"), P("dp", "head"), P("head", "dp", None))
    return jax.shard_map(body, mesh=mesh, in_specs=in_specs, out_specs=out_specs, check_vma=False)
```

```python
import math

import jax
import jax.numpy as jnp
import numpy as np
from jax import lax
from jax.experimental import pallas as pl
from jax.experimental.pallas import tpu as pltpu
from jax.sharding import PartitionSpec as P

HD = 128
QH_DEV = 4
QC = QH_DEV * HD
COLS = 768
ROWS = 256
SPAN = 2
N_DP = 96
N_LOW = 4
HALF = HD // 2


EPSILON = 1e-06
THETA = 1000000.0
STRETCH = 0.25
SCALE = 1.0 / math.sqrt(HD)


NY, NX, NZ = 8, 4, 3
D = 2048
CA = 1024
CB = D - CA
CH = CB // 2
MESH = pl.DeviceIdType.MESH
BF, F32 = jnp.bfloat16, jnp.float32


class Links:
    def __init__(self, send_sem, recv_sem):
        self.send_sem, self.recv_sem = send_sem, recv_sem
        self.sent = []

    def send(self, src, dst, target):
        n = len(self.sent)
        copy = pltpu.make_async_remote_copy(
            src_ref=src, dst_ref=dst, send_sem=self.send_sem.at[n], recv_sem=self.recv_sem.at[n],
            device_id=target, device_id_type=MESH)
        copy.start()
        self.sent.append(copy)
        return copy

    def finish(self):
        for copy in self.sent:
            copy.wait_send()


def rounds(sequences):
    live = list(sequences)
    while live:
        still = []
        for s in live:
            if next(s, 0) is None:
                still.append(s)
                yield
        live = still


def places():
    dp, head = lax.axis_index("dp"), lax.axis_index("head")
    return dp // (NX * NZ), (dp // NZ) % NX, dp % NZ, head


def at(y, x, z, head):
    return (((y + NY) % NY * NX + (x + NX) % NX) * NZ + (z + NZ) % NZ, head)


def ry(y):
    return (y + NY) % NY


def rx(x):
    return (x + NX) % NX


def rz(z):
    return (z + NZ) % NZ


def peers(y, x, z, head):
    out = [at(y + d, x, z, head) for d in (1, -1, 2, -2)]
    out += [at(y, x + d, z, head) for d in (1, 2, 3)]
    out += [at(y, x, z + d, head) for d in (1, 2)]
    return out


def enter(targets):
    barrier = pltpu.get_barrier_semaphore()
    for t in targets:
        pl.semaphore_signal(barrier, inc=1, device_id=t, device_id_type=MESH)
    pl.semaphore_wait(barrier, len(targets))


A = pl.ds(0, CA)
B = pl.ds(CA, CB)


TO_RIGHT = (0, 1, 2, 3)


def gather_rows(links, w, y, x, z, head):
    up, down, up2, down2 = (at(y + d, x, z, head) for d in (1, -1, 2, -2))
    right, left, across = (at(y, x + d, z, head) for d in (1, -1, 2))
    own = w.at[y, x, z]
    far = [links.send(own, own, at(y, x, z + d, head)) for d in (1, 2)]

    def arrived(copies):
        for c in copies:
            c.wait_recv()

    def seq_a(k):
        r = w.at[y, x, k, :, A]
        s = [links.send(r, r, t) for t in (right, left, across)]
        yield
        for step in range(4):
            arrived(s)
            s = []
            for sign, t, half in ((-1, up, 0), (1, down, NX // 2)):
                xs = pl.ds(0, NX) if step < 3 else pl.ds(half, NX // 2)
                r = w.at[ry(y + sign * step), xs, k, :, A]
                s.append(links.send(r, r, t))
            yield
        arrived(s)

    def seq_b(k):
        def shard(dy, dx, cols=B):
            return w.at[ry(y + dy), rx(x + dx), k, :, cols]

        def sideways(dys):
            out = []
            for dy in dys:
                r = shard(dy, 0)
                out.append((dy, links.send(r, r, right), links.send(r, r, left)))
            return out

        def onward(came):
            out = []
            for dy, from_left, from_right in came:
                from_left.wait_recv()
                from_right.wait_recv()
                r, t = (shard(dy, -1), right) if dy in TO_RIGHT else (shard(dy, 1), left)
                out.append(links.send(r, r, t))
            return out

        r = shard(0, 0)
        s = [links.send(r, r, t) for t in (up, down, up2, down2)]
        side = sideways((0,))
        yield
        arrived(s)
        s = []
        for dy, t, t2, half in ((-2, up, up2, pl.ds(CA, CH)), (2, down, down2, pl.ds(CA + CH, CH))):
            r, h = shard(dy, 0), shard(dy, 0, half)
            s += [links.send(r, r, t), links.send(h, h, t2)]
        side2 = sideways((2, -2, 1, -1))
        last = onward(side)
        yield
        arrived(s)
        side3 = sideways((3, -3, 4))
        last += onward(side2)
        yield
        last += onward(side3)
        yield
        arrived(last)

    def seq(d, kind):
        if d:
            yield
            if kind == 0:
                far[d - 1].wait_recv()
        yield from (seq_b, seq_a)[kind](rz(z - d))

    yield from rounds([seq(d, kind) for kind in (0, 1) for d in range(NZ)])


N_GATHER = 2 + 3 * (11 + 32)
N_SCATTER = 4 + 3 * (11 + 32)
SCATTER_LANDING = [
    pltpu.VMEM((NZ, 2, 4, NX, 8, CA), BF),
    pltpu.VMEM((NZ, 3, 8, CA), BF),
    pltpu.VMEM((NZ, NY, 8, CB), BF),
    pltpu.VMEM((NZ, 2, NY, 8, CB), BF),
    pltpu.VMEM((NZ, 8, 8, CB), BF),
    pltpu.VMEM((2, 8, D), BF),
]


def scatter_rows(links, g, landing, y, x, z, head):
    lay, lax_, lbx1, lbx2, lby, lz = landing
    up, down, up2, down2 = (at(y + d, x, z, head) for d in (1, -1, 2, -2))
    right, left, across = (at(y, x + d, z, head) for d in (1, -1, 2))

    def add(here, *theirs):
        total = g[here]
        for ref, idx in theirs:
            total = total + ref[idx]
        g[here] = total

    rows = slice(None)
    sent = []

    def finish(d, cols):
        if d:
            k = rz(z + d)
            sent.append(links.send(g.at[y, x, k, :, cols], lz.at[d - 1, :, cols], at(y, x, k, head)))

    def seq_a(d):
        k = rz(z + d)
        s = []
        for step in range(4):
            n = []
            for i, (sign, t) in enumerate(((1, up), (-1, down))):
                slab = ry(y + sign * (4 - step))
                half = pl.ds(i * (NX // 2), NX // 2)
                if step:
                    s[i].wait_recv()
                    xs = half if step == 1 else pl.ds(0, NX)
                    add((slab, xs, k, rows, A), (lay, (k, i, step - 1, xs)))
                xs = half if step == 0 else pl.ds(0, NX)
                n.append(links.send(g.at[slab, xs, k, :, A], lay.at[k, i, step, xs], t))
            s = n
            yield
        for c in s:
            c.wait_recv()
        add((y, pl.ds(0, NX), k, rows, A), (lay, (k, 0, 3)), (lay, (k, 1, 3)))
        s = [links.send(g.at[y, rx(x + e), k, :, A], lax_.at[k, e - 1], t)
             for e, t in ((1, right), (2, across), (3, left))]
        yield
        for c in s:
            c.wait_recv()
        add((y, x, k, rows, A), (lax_, (k, 0)), (lax_, (k, 1)), (lax_, (k, 2)))
        finish(d, A)

    def seq_b(d):
        k = rz(z + d)

        def first(dys):
            out = []
            for dy in dys:
                t = right if dy in TO_RIGHT else left
                out.append((dy, links.send(g.at[ry(y + dy), rx(x + 2), k, :, B], lbx1.at[k, ry(y + dy)], t)))
            return out

        def second(came):
            out = []
            for dy, c in came:
                ys = ry(y + dy)
                c.wait_recv()
                add((ys, rx(x + (1 if dy in TO_RIGHT else -1)), k, rows, B), (lbx1, (k, ys)))
                out.append((dy, [
                    links.send(g.at[ys, rx(x + sign), k, :, B], lbx2.at[k, i, ys], t)
                    for i, (sign, t) in enumerate(((1, right), (-1, left)))
                ]))
            return out

        def third(came):
            for dy, pair in came:
                ys = ry(y + dy)
                for c in pair:
                    c.wait_recv()
                add((ys, x, k, rows, B), (lbx2, (k, 0, ys)), (lbx2, (k, 1, ys)))

        def toward(dy, slot, t, cols=pl.ds(0, CB)):
            src = g.at[ry(y + dy), x, k, :, pl.ds(CA + cols.start, cols.size)]
            return links.send(src, lby.at[k, slot, :, cols], t)

        early, late = (4, 3, -3), (2, -2, 1, -1, 0)
        s1 = first(early)
        s2 = first(late)
        yield
        s1 = second(s1)
        yield
        s2 = second(s2)
        yield
        third(s1)
        h0, h1 = pl.ds(0, CH), pl.ds(CH, CH)
        s = [toward(3, 0, up), toward(-3, 1, down), toward(4, 2, up2, h0), toward(4, 3, down2, h1)]
        yield
        third(s2)
        n = [toward(1, 4, up), toward(-1, 5, down)]
        for c in s:
            c.wait_recv()
        add((ry(y + 2), x, k, rows, pl.ds(CA, CB)), (lby, (k, 0)))
        add((ry(y + 2), x, k, rows, pl.ds(CA, CH)), (lby, (k, 2, rows, h0)))
        add((ry(y - 2), x, k, rows, pl.ds(CA, CB)), (lby, (k, 1)))
        add((ry(y - 2), x, k, rows, pl.ds(CA + CH, CH)), (lby, (k, 3, rows, h1)))
        n += [toward(2, 6, up2), toward(-2, 7, down2)]
        yield
        for c in n:
            c.wait_recv()
        add((y, x, k, rows, B), *((lby, (k, slot)) for slot in (4, 5, 6, 7)))
        finish(d, B)

    def late(sequence):
        yield
        yield
        yield from sequence

    yield from rounds([seq_b(1), seq_b(2), seq_a(1), seq_a(2), late(seq_b(0)), late(seq_a(0))])
    for c in sent:
        c.wait_recv()
    yield


BLOCKS = (NY, NX, NZ, 8, D)
N_COPIES = N_GATHER + N_SCATTER + 4 + 5 + 7 + 1


def dot(a, b):
    return jnp.dot(a, b, preferred_element_type=F32)


def head_rows(h):
    return pl.ds(pl.multiple_of(h * HD, HD), HD)


def normalize(u, gain):
    factor = lax.rsqrt(jnp.mean(u * u, axis=0, keepdims=True) + EPSILON)
    return u * factor, factor


def rotate(n, cos, sin):
    a, b = n[:HALF], n[HALF:]
    return jnp.concatenate([a * cos - b * sin, b * cos + a * sin], axis=0)


def normalize_rotate_back(u, gain, cos, sin, grad):
    n, factor = normalize(u, gain)
    a, b = grad[:HALF], grad[HALF:]
    back = jnp.concatenate([a * cos + b * sin, b * cos - a * sin], axis=0) * gain
    return factor * (back - n * jnp.mean(back * n, axis=0, keepdims=True))


def layer_kernel(*refs):
    hbm_in, hbm_out, (w, g), landing = refs[:7], refs[7:10], refs[10:12], refs[12:18]
    tokens, query_gain, key_gain, frequency, first_row, cotangent = refs[18:24]
    results, local_sem, scratch = refs[24:27], refs[27], refs[28:]
    attended, token_grad, weight_grad = results
    (
        pair_out, pair_in, tokens_t, cot_t, tables, gains, proj_t, q_t, q_n, kv_t, kv_n, weight, denom,
        att_t, dq_t, dkv, d_out, d_pair, d_sum, d_in, gq_t, gq_n, part, tp, tp_pair, tp_low, token_sum, send_sem, recv_sem,
    ) = scratch
    dp = lax.axis_index("dp")
    y, x, z, head = places()
    low, core = head // 2, head % 2
    other = 1 - core
    sibling = (dp, 2 * low + other)
    ahead = [((dp + d) % N_DP, head) for d in (1, 2)]
    behind = [((dp + N_DP - d) % N_DP, head) for d in (1, 2)]
    lows = [(dp, (low + d) % N_LOW * 2 + core) for d in (1, 2, 3)]
    places_in = (tokens, w.at[y, x, z], query_gain, key_gain, frequency, first_row, cotangent)
    fetch = []
    for i in (1, 0, 2, 3, 4, 5, 6):
        source = hbm_in[i].at[0] if i == 1 else hbm_in[i]
        fetch.append(pltpu.make_async_copy(source, places_in[i], local_sem.at[i]))
        fetch[-1].start()

    def put(i):
        copy = pltpu.make_async_copy(results[i], hbm_out[i], local_sem.at[7 + i])
        copy.start()
        return copy

    enter(peers(y, x, z, head) + [sibling] + ahead + behind + lows)
    fetch[0].wait()
    links = Links(send_sem, recv_sem)
    w2, g2 = w.reshape(COLS, D), g.reshape(COLS, D)

    def prologue():
        for copy in fetch[1:]:
            copy.wait()
        square = (HD, HD)
        gains[0] = jnp.broadcast_to(query_gain[...], square).T
        gains[1] = jnp.broadcast_to(key_gain[...], square).T
        rate = jnp.broadcast_to(frequency[...], square).T[:HALF]
        rate = jnp.concatenate([rate, rate], axis=1)
        yield
        for c in range(0, D, ROWS):
            tokens_t[pl.ds(c, ROWS)] = tokens[:, pl.ds(c, ROWS)].T
            yield
        for c in range(0, QC, ROWS):
            cot_t[pl.ds(c, ROWS)] = cotangent[:, pl.ds(c, ROWS)].T
            yield
        for c in range(0, HALF, 16):
            place = (dp * ROWS + lax.broadcasted_iota(jnp.int32, (16, ROWS), 1)).astype(F32)
            angles = place * STRETCH * rate[c : c + 16]
            tables[0, pl.ds(c, 16)] = jnp.cos(angles)
            yield
            tables[1, pl.ds(c, 16)] = jnp.sin(angles)
            yield

    side = prologue()
    for i, _ in enumerate(gather_rows(links, w, y, x, z, head)):
        if i >= 5:
            next(side, None)
    for _ in side:
        pass

    def project(h, _):
        proj_t[head_rows(h)] = dot(w2[head_rows(h)], tokens_t[...])
        return 0

    lax.fori_loop(QH_DEV, COLS // HD, project, 0)

    def gain_of(i):
        return jnp.concatenate([gains[i], gains[i]], axis=1)

    def prepared(h, i):
        n, _ = normalize(proj_t[head_rows(h)], None)
        return rotate(n * gain_of(i), tables[0], tables[1]).astype(BF)

    kv_t[0, 0] = prepared(QH_DEV, 1)
    kv_t[0, 1] = proj_t[pl.ds(QC + HD, HD)].astype(BF)
    halo = [links.send(kv_t.at[0, core], kv_t.at[d, core], ahead[d - 1]) for d in (1, 2)]

    def natural(j):
        kv_n[j, 0] = kv_t[j, 0].T
        kv_n[j, 1] = kv_t[j, 1].T

    natural(0)
    lax.fori_loop(0, QH_DEV, project, 0)

    def prepare_query(h, _):
        turned = prepared(h, 0)
        q_t[head_rows(h)] = turned
        q_n[h] = turned.T
        return 0

    lax.fori_loop(0, QH_DEV, prepare_query, 0)

    row = lax.broadcasted_iota(jnp.int32, (ROWS, ROWS), 1)
    key = lax.broadcasted_iota(jnp.int32, (ROWS, ROWS), 0)

    def forward(j, h):
        key_place = (dp - j) * ROWS + key
        visible = key_place >= first_row[...]
        if j == 0:
            visible = visible & (key <= row)
        score = dot(kv_n[j, 0], q_t[head_rows(h)]) * SCALE
        seen = jnp.where(visible, jnp.exp(score), 0.0)
        weight[h, j] = seen
        return jnp.sum(seen, axis=0, keepdims=True), dot(kv_t[j, 1], seen.astype(BF))

    def own_forward(h, _):
        denom[h], att_t[head_rows(h)] = forward(0, h)
        return 0

    lax.fori_loop(0, QH_DEV, own_forward, 0)

    pair = []
    for d in (1, 2):
        halo[d - 1].wait_recv()
        pair.append(links.send(kv_t.at[d, core], kv_t.at[d, core], sibling))
    for d in (1, 2):
        pair[d - 1].wait_recv()
        natural(d)

    def backward(j, h, inverse, delta):
        probability = weight[h, j] * inverse
        grad_prob = dot(kv_n[j, 1], cot_t[head_rows(h)])
        grad_score = (probability * (grad_prob - delta) * SCALE).astype(BF)
        dk = dot(grad_score, q_n[h])
        dv = dot(probability.astype(BF), cotangent[:, head_rows(h)])
        return dot(kv_t[j, 0], grad_score), dk, dv

    dkv[...] = jnp.zeros_like(dkv)

    def far(h, _):
        total, summed = denom[h], att_t[head_rows(h)]
        for j in (1, 2):
            more, moved = forward(j, h)
            total = total + more
            summed = summed + moved
        inverse = 1.0 / total
        out = (summed * inverse).astype(BF)
        attended[:, head_rows(h)] = out.T
        delta = jnp.sum(cot_t[head_rows(h)].astype(F32) * out.astype(F32), axis=0, keepdims=True)
        denom[h] = inverse
        att_t[head_rows(h)] = jnp.broadcast_to(delta, (HD, ROWS))
        dq = None
        for j in (1, 2):
            more, dk, dv = backward(j, h, inverse, delta)
            dq = more if dq is None else dq + more
            dkv[j, 0] += dk
            dkv[j, 1] += dv
        dq_t[head_rows(h)] = dq
        return 0

    lax.fori_loop(0, QH_DEV, far, 0)

    put_attended = put(0)

    def to_pair(j):
        d_out[j] = dkv[j, other].astype(BF)
        return links.send(d_out.at[j], d_pair.at[j], sibling)

    back = [to_pair(j) for j in (1, 2)]

    def near(h, _):
        dq, dk, dv = backward(0, h, denom[h], att_t[pl.ds(pl.multiple_of(h * HD, HD), 8)][:1])
        dkv[0, 0] += dk
        dkv[0, 1] += dv
        grad = dq_t[head_rows(h)] + dq
        back_t = normalize_rotate_back(proj_t[head_rows(h)], gain_of(0), tables[0], tables[1], grad).astype(BF)
        gq_t[head_rows(h)] = back_t
        gq_n[:, head_rows(h)] = back_t.T
        return 0

    for j in (1, 2):
        back[j - 1].wait_recv()
        d_sum[j - 1] = (dkv[j, core] + d_pair[j].astype(F32)).astype(BF)
        back[j - 1] = links.send(d_sum.at[j - 1], d_in.at[j - 1], behind[j - 1])
    lax.fori_loop(0, QH_DEV, near, 0)
    back_own = to_pair(0)

    def own_grads(h, _):
        g2[head_rows(h)] = dot(gq_t[head_rows(h)], tokens[...]).astype(BF)
        return 0

    lax.fori_loop(0, QH_DEV, own_grads, 0)
    mine = pl.ds(pl.multiple_of(QC + core * HD, HD), HD)
    theirs = pl.ds(pl.multiple_of(QC + other * HD, HD), HD)
    g2[theirs] = jnp.zeros((HD, D), BF)

    def token_part(i, _):
        cols = pl.ds(pl.multiple_of(i * ROWS, ROWS), ROWS)
        part[i] = dot(gq_n[...], w2[pl.ds(0, QC), cols])
        return 0

    lax.fori_loop(0, 8, token_part, 0)

    back_own.wait_recv()
    total = dkv[0, core] + d_pair[0].astype(F32)
    for j in (0, 1):
        back[j].wait_recv()
        total = total + d_in[j].astype(F32)
    total = total.T
    turned = normalize_rotate_back(proj_t[pl.ds(QC, HD)], gain_of(1), tables[0], tables[1], total)
    total = jnp.where(core == 0, turned, total).astype(BF)
    gk_n = total.T
    g2[mine] = dot(total, tokens[...]).astype(BF)

    low_copies = []

    def token_rest():
        swap = []
        for i in range(8):
            block = i // 2 * 2 + (other if i % 2 == 0 else core)
            cols = pl.ds(pl.multiple_of(block * ROWS, ROWS), ROWS)
            tp[block] = (part[block] + dot(gk_n, w2[mine, cols])).astype(BF)
            if i % 2 == 0:
                swap.append(links.send(tp.at[block], tp_pair.at[i // 2], sibling))
            if i % 2:
                yield
        for d in (1, 2, 3):
            place = (low + d) % N_LOW
            block = place * 2 + core
            if d == 1:
                for c in swap:
                    c.wait_recv()
            tp[block] = tp[block] + tp_pair[place]
            low_copies.append(links.send(tp.at[block], tp_low.at[d - 1], lows[d - 1]))
            yield
        token_sum[...] = tp[head].astype(F32) + tp_pair[low].astype(F32)

    side = token_rest()
    for i, _ in enumerate(scatter_rows(links, g, landing, y, x, z, head)):
        if i >= 3:
            next(side, None)
    for _ in side:
        pass
    own = g[y, x, z].astype(F32) + landing[5][0].astype(F32) + landing[5][1].astype(F32)
    pair_out[...] = own.astype(BF)
    last = links.send(pair_out, pair_in, sibling)
    total = token_sum[...]
    for d in range(3):
        low_copies[d].wait_recv()
        total = total + tp_low[d].astype(F32)
    token_grad[...] = total.astype(BF)
    put_token = put(1)
    last.wait_recv()
    weight_grad[0] = own + jnp.where(dp * 8 >= QC, pair_in[...].astype(F32), 0.0)
    put_weight = put(2)
    links.finish()
    put_attended.wait()
    put_token.wait()
    put_weight.wait()


def body(tokens, weights, query_gain, key_gain, first_row, cotangent):
    channel = np.arange(HALF, dtype=np.float64)
    rates = (THETA ** (-2.0 * channel / HD)).astype(np.float32)
    frequency = jnp.asarray(np.concatenate([rates, rates])[None])
    return pl.pallas_call(
        layer_kernel,
        out_shape=(
            jax.ShapeDtypeStruct((ROWS, QC), BF),
            jax.ShapeDtypeStruct((ROWS, D // 8), BF),
            jax.ShapeDtypeStruct((1, 8, D), F32),
        ),
        in_specs=[pl.BlockSpec(memory_space=pl.ANY)] * 7,
        out_specs=[pl.BlockSpec(memory_space=pl.ANY)] * 3,
        scratch_shapes=[
            pltpu.VMEM(BLOCKS, BF),
            pltpu.VMEM(BLOCKS, BF),
            *SCATTER_LANDING,
            pltpu.VMEM((ROWS, D), BF),
            pltpu.VMEM((1, HD), F32),
            pltpu.VMEM((1, HD), F32),
            pltpu.VMEM((1, HD), F32),
            pltpu.VMEM((1, ROWS), jnp.int32),
            pltpu.VMEM((ROWS, QC), BF),
            pltpu.VMEM((ROWS, QC), BF),
            pltpu.VMEM((ROWS, D // 8), BF),
            pltpu.VMEM((1, 8, D), F32),
            pltpu.SemaphoreType.DMA((10,)),
            pltpu.VMEM((8, D), BF),
            pltpu.VMEM((8, D), BF),
            pltpu.VMEM((D, ROWS), BF),
            pltpu.VMEM((QC, ROWS), BF),
            pltpu.VMEM((2, HALF, ROWS), F32),
            pltpu.VMEM((2, HD, HD), F32),
            pltpu.VMEM((COLS, ROWS), F32),
            pltpu.VMEM((QC, ROWS), BF),
            pltpu.VMEM((QH_DEV, ROWS, HD), BF),
            pltpu.VMEM((SPAN + 1, 2, HD, ROWS), BF),
            pltpu.VMEM((SPAN + 1, 2, ROWS, HD), BF),
            pltpu.VMEM((QH_DEV, SPAN + 1, ROWS, ROWS), F32),
            pltpu.VMEM((QH_DEV, 1, ROWS), F32),
            pltpu.VMEM((QC, ROWS), F32),
            pltpu.VMEM((QC, ROWS), F32),
            pltpu.VMEM((SPAN + 1, 2, ROWS, HD), F32),
            pltpu.VMEM((SPAN + 1, ROWS, HD), BF),
            pltpu.VMEM((SPAN + 1, ROWS, HD), BF),
            pltpu.VMEM((SPAN, ROWS, HD), BF),
            pltpu.VMEM((SPAN, ROWS, HD), BF),
            pltpu.VMEM((QC, ROWS), BF),
            pltpu.VMEM((ROWS, QC), BF),
            pltpu.VMEM((8, ROWS, ROWS), F32),
            pltpu.VMEM((8, ROWS, ROWS), BF),
            pltpu.VMEM((N_LOW, ROWS, ROWS), BF),
            pltpu.VMEM((N_LOW - 1, ROWS, ROWS), BF),
            pltpu.VMEM((ROWS, ROWS), F32),
            pltpu.SemaphoreType.DMA((N_COPIES,)),
            pltpu.SemaphoreType.DMA((N_COPIES,)),
        ],
        compiler_params=pltpu.CompilerParams(
            collective_id=1, has_side_effects=True, vmem_limit_bytes=63 << 20
        ),
        cost_estimate=pl.CostEstimate(flops=4 * 10**9, bytes_accessed=4 << 20, transcendentals=10**6),
        name="masked_attention_layer",
    )(
        tokens,
        weights,
        query_gain.reshape(1, HD),
        key_gain.reshape(1, HD),
        frequency,
        first_row.reshape(1, ROWS),
        cotangent,
    )


def solution(mesh):
    in_specs = (P("dp", None), P("head", "dp", None), P(), P(), P("dp"), P("dp", "head"))
    out_specs = (P("dp", "head"), P("dp", "head"), P("head", "dp", None))
    return jax.shard_map(body, mesh=mesh, in_specs=in_specs, out_specs=out_specs, check_vma=False)
```

```python
import math

import jax
import jax.numpy as jnp
import numpy as np
from jax import lax
from jax.experimental import pallas as pl
from jax.experimental.pallas import tpu as pltpu
from jax.sharding import PartitionSpec as P

HD = 128
QH_DEV = 4
QC = QH_DEV * HD
COLS = 768
ROWS = 256
SPAN = 2
N_DP = 96
N_LOW = 4
HALF = HD // 2


EPSILON = 1e-06
THETA = 1000000.0
STRETCH = 0.25
SCALE = 1.0 / math.sqrt(HD)


NY, NX, NZ = 8, 4, 3
D = 2048
CA = 768
CB = D - CA
CH = CB // 2
MESH = pl.DeviceIdType.MESH
BF, F32 = jnp.bfloat16, jnp.float32


class Links:
    def __init__(self, send_sem, recv_sem):
        self.send_sem, self.recv_sem = send_sem, recv_sem
        self.sent = []

    def send(self, src, dst, target):
        n = len(self.sent)
        copy = pltpu.make_async_remote_copy(
            src_ref=src, dst_ref=dst, send_sem=self.send_sem.at[n], recv_sem=self.recv_sem.at[n],
            device_id=target, device_id_type=MESH)
        copy.start()
        self.sent.append(copy)
        return copy

    def finish(self):
        for copy in self.sent:
            copy.wait_send()


def rounds(sequences):
    live = list(sequences)
    while live:
        still = []
        for s in live:
            if next(s, 0) is None:
                still.append(s)
                yield
        live = still


def places():
    dp, head = lax.axis_index("dp"), lax.axis_index("head")
    return dp // (NX * NZ), (dp // NZ) % NX, dp % NZ, head


def at(y, x, z, head):
    return (((y + NY) % NY * NX + (x + NX) % NX) * NZ + (z + NZ) % NZ, head)


def ry(y):
    return (y + NY) % NY


def rx(x):
    return (x + NX) % NX


def rz(z):
    return (z + NZ) % NZ


def peers(y, x, z, head):
    out = [at(y + d, x, z, head) for d in (1, -1, 2, -2)]
    out += [at(y, x + d, z, head) for d in (1, 2, 3)]
    out += [at(y, x, z + d, head) for d in (1, 2)]
    return out


def enter(targets):
    barrier = pltpu.get_barrier_semaphore()
    for t in targets:
        pl.semaphore_signal(barrier, inc=1, device_id=t, device_id_type=MESH)
    pl.semaphore_wait(barrier, len(targets))


A = pl.ds(0, CA)
B = pl.ds(CA, CB)


TO_RIGHT = (0, 1, 2, 3)


def gather_rows(links, w, y, x, z, head):
    up, down, up2, down2 = (at(y + d, x, z, head) for d in (1, -1, 2, -2))
    right, left, across = (at(y, x + d, z, head) for d in (1, -1, 2))
    own = w.at[y, x, z]
    far = [links.send(own, own, at(y, x, z + d, head)) for d in (1, 2)]

    def arrived(copies):
        for c in copies:
            c.wait_recv()

    def seq_a(k):
        r = w.at[y, x, k, :, A]
        s = [links.send(r, r, t) for t in (right, left, across)]
        yield
        for step in range(3):
            arrived(s)
            s = []
            for sign, t, t2, half in ((-1, up, up2, 0), (1, down, down2, NX // 2)):
                slab = ry(y + sign * step)
                r = w.at[slab, :, k, :, A]
                s.append(links.send(r, r, t))
                if step == 2:
                    r = w.at[slab, pl.ds(half, NX // 2), k, :, A]
                    s.append(links.send(r, r, t2))
            yield
        arrived(s)

    def seq_b(k):
        def shard(dy, dx, cols=B):
            return w.at[ry(y + dy), rx(x + dx), k, :, cols]

        def sideways(dys):
            out = []
            for dy in dys:
                r = shard(dy, 0)
                out.append((dy, links.send(r, r, right), links.send(r, r, left)))
            return out

        def onward(came):
            out = []
            for dy, from_left, from_right in came:
                from_left.wait_recv()
                from_right.wait_recv()
                r, t = (shard(dy, -1), right) if dy in TO_RIGHT else (shard(dy, 1), left)
                out.append(links.send(r, r, t))
            return out

        r = shard(0, 0)
        s = [links.send(r, r, t) for t in (up, down, up2, down2)]
        side = sideways((0,))
        yield
        arrived(s)
        s = []
        for dy, t, t2, half in ((-2, up, up2, pl.ds(CA, CH)), (2, down, down2, pl.ds(CA + CH, CH))):
            r, h = shard(dy, 0), shard(dy, 0, half)
            s += [links.send(r, r, t), links.send(h, h, t2)]
        side2 = sideways((2, -2, 1, -1))
        last = onward(side)
        yield
        arrived(s)
        side3 = sideways((3, -3, 4))
        last += onward(side2)
        yield
        last += onward(side3)
        yield
        arrived(last)

    def seq(d, kind):
        if d:
            yield
            if kind == 0:
                far[d - 1].wait_recv()
        yield from (seq_b, seq_a)[kind](rz(z - d))

    yield from rounds([seq(d, kind) for kind in (0, 1) for d in range(NZ)])


N_GATHER = 2 + 3 * (11 + 32)
N_SCATTER = 4 + 3 * (11 + 32)
SCATTER_LANDING = [
    pltpu.VMEM((NZ, 2, 4, NX, 8, CA), BF),
    pltpu.VMEM((NZ, 3, 8, CA), BF),
    pltpu.VMEM((NZ, NY, 8, CB), BF),
    pltpu.VMEM((NZ, 2, NY, 8, CB), BF),
    pltpu.VMEM((NZ, 8, 8, CB), BF),
    pltpu.VMEM((2, 8, D), BF),
]


def scatter_rows(links, g, landing, y, x, z, head):
    lay, lax_, lbx1, lbx2, lby, lz = landing
    up, down, up2, down2 = (at(y + d, x, z, head) for d in (1, -1, 2, -2))
    right, left, across = (at(y, x + d, z, head) for d in (1, -1, 2))

    def add(here, *theirs):
        total = g[here]
        for ref, idx in theirs:
            total = total + ref[idx]
        g[here] = total

    rows = slice(None)
    sent = []

    def finish(d, cols):
        if d:
            k = rz(z + d)
            sent.append(links.send(g.at[y, x, k, :, cols], lz.at[d - 1, :, cols], at(y, x, k, head)))

    def seq_a(d):
        k = rz(z + d)
        s = []
        twice = []
        for step in range(3):
            n = []
            for i, (sign, t, t2) in enumerate(((1, up, up2), (-1, down, down2))):
                slab = ry(y + sign * (3 - step))
                half = pl.ds(i * (NX // 2), NX // 2)
                if step:
                    s[i].wait_recv()
                    add((slab, pl.ds(0, NX), k, rows, A), (lay, (k, i, step - 1)))
                if step == 1:
                    twice[i].wait_recv()
                    add((slab, half, k, rows, A), (lay, (k, i, 3, half)))
                n.append(links.send(g.at[slab, :, k, :, A], lay.at[k, i, step], t))
                if step == 0:
                    twice.append(links.send(g.at[ry(y + 4), half, k, :, A], lay.at[k, i, 3, half], t2))
            s = n
            yield
        for c in s:
            c.wait_recv()
        add((y, pl.ds(0, NX), k, rows, A), (lay, (k, 0, 2)), (lay, (k, 1, 2)))
        s = [links.send(g.at[y, rx(x + e), k, :, A], lax_.at[k, e - 1], t)
             for e, t in ((1, right), (2, across), (3, left))]
        yield
        for c in s:
            c.wait_recv()
        add((y, x, k, rows, A), (lax_, (k, 0)), (lax_, (k, 1)), (lax_, (k, 2)))
        finish(d, A)

    def seq_b(d):
        k = rz(z + d)

        def first(dys):
            out = []
            for dy in dys:
                t = right if dy in TO_RIGHT else left
                out.append((dy, links.send(g.at[ry(y + dy), rx(x + 2), k, :, B], lbx1.at[k, ry(y + dy)], t)))
            return out

        def second(came):
            out = []
            for dy, c in came:
                ys = ry(y + dy)
                c.wait_recv()
                add((ys, rx(x + (1 if dy in TO_RIGHT else -1)), k, rows, B), (lbx1, (k, ys)))
                out.append((dy, [
                    links.send(g.at[ys, rx(x + sign), k, :, B], lbx2.at[k, i, ys], t)
                    for i, (sign, t) in enumerate(((1, right), (-1, left)))
                ]))
            return out

        def third(came):
            for dy, pair in came:
                ys = ry(y + dy)
                for c in pair:
                    c.wait_recv()
                add((ys, x, k, rows, B), (lbx2, (k, 0, ys)), (lbx2, (k, 1, ys)))

        def toward(dy, slot, t, cols=pl.ds(0, CB)):
            src = g.at[ry(y + dy), x, k, :, pl.ds(CA + cols.start, cols.size)]
            return links.send(src, lby.at[k, slot, :, cols], t)

        early, late = (4, 3, -3), (2, -2, 1, -1, 0)
        s1 = first(early)
        s2 = first(late)
        yield
        s1 = second(s1)
        yield
        s2 = second(s2)
        yield
        third(s1)
        h0, h1 = pl.ds(0, CH), pl.ds(CH, CH)
        s = [toward(3, 0, up), toward(-3, 1, down), toward(4, 2, up2, h0), toward(4, 3, down2, h1)]
        yield
        third(s2)
        n = [toward(1, 4, up), toward(-1, 5, down)]
        for c in s:
            c.wait_recv()
        add((ry(y + 2), x, k, rows, pl.ds(CA, CB)), (lby, (k, 0)))
        add((ry(y + 2), x, k, rows, pl.ds(CA, CH)), (lby, (k, 2, rows, h0)))
        add((ry(y - 2), x, k, rows, pl.ds(CA, CB)), (lby, (k, 1)))
        add((ry(y - 2), x, k, rows, pl.ds(CA + CH, CH)), (lby, (k, 3, rows, h1)))
        n += [toward(2, 6, up2), toward(-2, 7, down2)]
        yield
        for c in n:
            c.wait_recv()
        add((y, x, k, rows, B), *((lby, (k, slot)) for slot in (4, 5, 6, 7)))
        finish(d, B)

    def late(sequence):
        yield
        yield
        yield from sequence

    yield from rounds([seq_b(1), seq_b(2), seq_a(1), seq_a(2), late(seq_b(0)), late(seq_a(0))])
    for c in sent:
        c.wait_recv()
    yield


BLOCKS = (NY, NX, NZ, 8, D)
N_COPIES = N_GATHER + N_SCATTER + 4 + 5 + 7 + 1


def dot(a, b):
    return jnp.dot(a, b, preferred_element_type=F32)


def head_rows(h):
    return pl.ds(pl.multiple_of(h * HD, HD), HD)


def normalize(u, gain):
    factor = lax.rsqrt(jnp.mean(u * u, axis=0, keepdims=True) + EPSILON)
    return u * factor, factor


def rotate(n, cos, sin):
    a, b = n[:HALF], n[HALF:]
    return jnp.concatenate([a * cos - b * sin, b * cos + a * sin], axis=0)


def normalize_rotate_back(u, gain, cos, sin, grad):
    n, factor = normalize(u, gain)
    a, b = grad[:HALF], grad[HALF:]
    back = jnp.concatenate([a * cos + b * sin, b * cos - a * sin], axis=0) * gain
    return factor * (back - n * jnp.mean(back * n, axis=0, keepdims=True))


def layer_kernel(*refs):
    hbm_in, hbm_out, (w, g), landing = refs[:7], refs[7:10], refs[10:12], refs[12:18]
    tokens, query_gain, key_gain, frequency, first_row, cotangent = refs[18:24]
    results, local_sem, scratch = refs[24:27], refs[27], refs[28:]
    attended, token_grad, weight_grad = results
    (
        pair_out, pair_in, tokens_t, cot_t, tables, gains, proj_t, q_t, q_n, kv_t, kv_n, weight, denom,
        att_t, dq_t, dkv, d_out, d_pair, d_sum, d_in, gq_t, gq_n, part, tp, tp_pair, tp_low, token_sum, send_sem, recv_sem,
    ) = scratch
    dp = lax.axis_index("dp")
    y, x, z, head = places()
    low, core = head // 2, head % 2
    other = 1 - core
    sibling = (dp, 2 * low + other)
    ahead = [((dp + d) % N_DP, head) for d in (1, 2)]
    behind = [((dp + N_DP - d) % N_DP, head) for d in (1, 2)]
    lows = [(dp, (low + d) % N_LOW * 2 + core) for d in (1, 2, 3)]
    places_in = (tokens, w.at[y, x, z], query_gain, key_gain, frequency, first_row, cotangent)
    fetch = []
    for i in (1, 0, 2, 3, 4, 5, 6):
        source = hbm_in[i].at[0] if i == 1 else hbm_in[i]
        fetch.append(pltpu.make_async_copy(source, places_in[i], local_sem.at[i]))
        fetch[-1].start()

    def put(i):
        copy = pltpu.make_async_copy(results[i], hbm_out[i], local_sem.at[7 + i])
        copy.start()
        return copy

    enter(peers(y, x, z, head) + [sibling] + ahead + behind + lows)
    fetch[0].wait()
    links = Links(send_sem, recv_sem)
    w2, g2 = w.reshape(COLS, D), g.reshape(COLS, D)

    def prologue():
        for copy in fetch[1:]:
            copy.wait()
        square = (HD, HD)
        gains[0] = jnp.broadcast_to(query_gain[...], square).T
        gains[1] = jnp.broadcast_to(key_gain[...], square).T
        rate = jnp.broadcast_to(frequency[...], square).T[:HALF]
        rate = jnp.concatenate([rate, rate], axis=1)
        yield
        for c in range(0, D, ROWS):
            tokens_t[pl.ds(c, ROWS)] = tokens[:, pl.ds(c, ROWS)].T
            yield
        for c in range(0, QC, ROWS):
            cot_t[pl.ds(c, ROWS)] = cotangent[:, pl.ds(c, ROWS)].T
            yield
        for c in range(0, HALF, 16):
            place = (dp * ROWS + lax.broadcasted_iota(jnp.int32, (16, ROWS), 1)).astype(F32)
            angles = place * STRETCH * rate[c : c + 16]
            tables[0, pl.ds(c, 16)] = jnp.cos(angles)
            yield
            tables[1, pl.ds(c, 16)] = jnp.sin(angles)
            yield

    side = prologue()
    for i, _ in enumerate(gather_rows(links, w, y, x, z, head)):
        if i >= 5:
            next(side, None)
    for _ in side:
        pass

    def project(h, _):
        proj_t[head_rows(h)] = dot(w2[head_rows(h)], tokens_t[...])
        return 0

    lax.fori_loop(QH_DEV, COLS // HD, project, 0)

    def gain_of(i):
        return jnp.concatenate([gains[i], gains[i]], axis=1)

    def prepared(h, i):
        n, _ = normalize(proj_t[head_rows(h)], None)
        return rotate(n * gain_of(i), tables[0], tables[1]).astype(BF)

    kv_t[0, 0] = prepared(QH_DEV, 1)
    kv_t[0, 1] = proj_t[pl.ds(QC + HD, HD)].astype(BF)
    halo = [links.send(kv_t.at[0, core], kv_t.at[d, core], ahead[d - 1]) for d in (1, 2)]

    def natural(j):
        kv_n[j, 0] = kv_t[j, 0].T
        kv_n[j, 1] = kv_t[j, 1].T

    natural(0)
    lax.fori_loop(0, QH_DEV, project, 0)

    def prepare_query(h, _):
        turned = prepared(h, 0)
        q_t[head_rows(h)] = turned
        q_n[h] = turned.T
        return 0

    lax.fori_loop(0, QH_DEV, prepare_query, 0)

    row = lax.broadcasted_iota(jnp.int32, (ROWS, ROWS), 1)
    key = lax.broadcasted_iota(jnp.int32, (ROWS, ROWS), 0)

    def forward(j, h):
        key_place = (dp - j) * ROWS + key
        visible = key_place >= first_row[...]
        if j == 0:
            visible = visible & (key <= row)
        score = dot(kv_n[j, 0], q_t[head_rows(h)]) * SCALE
        seen = jnp.where(visible, jnp.exp(score), 0.0)
        weight[h, j] = seen
        return jnp.sum(seen, axis=0, keepdims=True), dot(kv_t[j, 1], seen.astype(BF))

    def own_forward(h, _):
        denom[h], att_t[head_rows(h)] = forward(0, h)
        return 0

    lax.fori_loop(0, QH_DEV, own_forward, 0)

    pair = []
    for d in (1, 2):
        halo[d - 1].wait_recv()
        pair.append(links.send(kv_t.at[d, core], kv_t.at[d, core], sibling))
    for d in (1, 2):
        pair[d - 1].wait_recv()
        natural(d)

    def backward(j, h, inverse, delta):
        probability = weight[h, j] * inverse
        grad_prob = dot(kv_n[j, 1], cot_t[head_rows(h)])
        grad_score = (probability * (grad_prob - delta) * SCALE).astype(BF)
        dk = dot(grad_score, q_n[h])
        dv = dot(probability.astype(BF), cotangent[:, head_rows(h)])
        return dot(kv_t[j, 0], grad_score), dk, dv

    dkv[...] = jnp.zeros_like(dkv)

    def far(h, _):
        total, summed = denom[h], att_t[head_rows(h)]
        for j in (1, 2):
            more, moved = forward(j, h)
            total = total + more
            summed = summed + moved
        inverse = 1.0 / total
        out = (summed * inverse).astype(BF)
        attended[:, head_rows(h)] = out.T
        delta = jnp.sum(cot_t[head_rows(h)].astype(F32) * out.astype(F32), axis=0, keepdims=True)
        denom[h] = inverse
        att_t[head_rows(h)] = jnp.broadcast_to(delta, (HD, ROWS))
        dq = None
        for j in (1, 2):
            more, dk, dv = backward(j, h, inverse, delta)
            dq = more if dq is None else dq + more
            dkv[j, 0] += dk
            dkv[j, 1] += dv
        dq_t[head_rows(h)] = dq
        return 0

    lax.fori_loop(0, QH_DEV, far, 0)

    put_attended = put(0)

    def to_pair(j):
        d_out[j] = dkv[j, other].astype(BF)
        return links.send(d_out.at[j], d_pair.at[j], sibling)

    back = [to_pair(j) for j in (1, 2)]

    def near(h, _):
        dq, dk, dv = backward(0, h, denom[h], att_t[pl.ds(pl.multiple_of(h * HD, HD), 8)][:1])
        dkv[0, 0] += dk
        dkv[0, 1] += dv
        grad = dq_t[head_rows(h)] + dq
        back_t = normalize_rotate_back(proj_t[head_rows(h)], gain_of(0), tables[0], tables[1], grad).astype(BF)
        gq_t[head_rows(h)] = back_t
        gq_n[:, head_rows(h)] = back_t.T
        return 0

    for j in (1, 2):
        back[j - 1].wait_recv()
        d_sum[j - 1] = (dkv[j, core] + d_pair[j].astype(F32)).astype(BF)
        back[j - 1] = links.send(d_sum.at[j - 1], d_in.at[j - 1], behind[j - 1])
    lax.fori_loop(0, QH_DEV, near, 0)
    back_own = to_pair(0)

    def own_grads(h, _):
        g2[head_rows(h)] = dot(gq_t[head_rows(h)], tokens[...]).astype(BF)
        return 0

    lax.fori_loop(0, QH_DEV, own_grads, 0)
    mine = pl.ds(pl.multiple_of(QC + core * HD, HD), HD)
    theirs = pl.ds(pl.multiple_of(QC + other * HD, HD), HD)
    g2[theirs] = jnp.zeros((HD, D), BF)

    def token_part(i, _):
        cols = pl.ds(pl.multiple_of(i * ROWS, ROWS), ROWS)
        part[i] = dot(gq_n[...], w2[pl.ds(0, QC), cols])
        return 0

    lax.fori_loop(0, 8, token_part, 0)

    back_own.wait_recv()
    total = dkv[0, core] + d_pair[0].astype(F32)
    for j in (0, 1):
        back[j].wait_recv()
        total = total + d_in[j].astype(F32)
    total = total.T
    turned = normalize_rotate_back(proj_t[pl.ds(QC, HD)], gain_of(1), tables[0], tables[1], total)
    total = jnp.where(core == 0, turned, total).astype(BF)
    gk_n = total.T
    g2[mine] = dot(total, tokens[...]).astype(BF)

    low_copies = []

    def token_rest():
        swap = []
        for i in range(8):
            block = i // 2 * 2 + (other if i % 2 == 0 else core)
            cols = pl.ds(pl.multiple_of(block * ROWS, ROWS), ROWS)
            tp[block] = (part[block] + dot(gk_n, w2[mine, cols])).astype(BF)
            if i % 2 == 0:
                swap.append(links.send(tp.at[block], tp_pair.at[i // 2], sibling))
            if i % 2:
                yield
        for d in (1, 2, 3):
            place = (low + d) % N_LOW
            block = place * 2 + core
            if d == 1:
                for c in swap:
                    c.wait_recv()
            tp[block] = tp[block] + tp_pair[place]
            low_copies.append(links.send(tp.at[block], tp_low.at[d - 1], lows[d - 1]))
            yield
        token_sum[...] = tp[head].astype(F32) + tp_pair[low].astype(F32)

    side = token_rest()
    for i, _ in enumerate(scatter_rows(links, g, landing, y, x, z, head)):
        if i >= 3:
            next(side, None)
    for _ in side:
        pass
    own = g[y, x, z].astype(F32) + landing[5][0].astype(F32) + landing[5][1].astype(F32)
    pair_out[...] = own.astype(BF)
    last = links.send(pair_out, pair_in, sibling)
    total = token_sum[...]
    for d in range(3):
        low_copies[d].wait_recv()
        total = total + tp_low[d].astype(F32)
    token_grad[...] = total.astype(BF)
    put_token = put(1)
    last.wait_recv()
    weight_grad[0] = own + jnp.where(dp * 8 >= QC, pair_in[...].astype(F32), 0.0)
    put_weight = put(2)
    links.finish()
    put_attended.wait()
    put_token.wait()
    put_weight.wait()


def body(tokens, weights, query_gain, key_gain, first_row, cotangent):
    channel = np.arange(HALF, dtype=np.float64)
    rates = (THETA ** (-2.0 * channel / HD)).astype(np.float32)
    frequency = jnp.asarray(np.concatenate([rates, rates])[None])
    return pl.pallas_call(
        layer_kernel,
        out_shape=(
            jax.ShapeDtypeStruct((ROWS, QC), BF),
            jax.ShapeDtypeStruct((ROWS, D // 8), BF),
            jax.ShapeDtypeStruct((1, 8, D), F32),
        ),
        in_specs=[pl.BlockSpec(memory_space=pl.ANY)] * 7,
        out_specs=[pl.BlockSpec(memory_space=pl.ANY)] * 3,
        scratch_shapes=[
            pltpu.VMEM(BLOCKS, BF),
            pltpu.VMEM(BLOCKS, BF),
            *SCATTER_LANDING,
            pltpu.VMEM((ROWS, D), BF),
            pltpu.VMEM((1, HD), F32),
            pltpu.VMEM((1, HD), F32),
            pltpu.VMEM((1, HD), F32),
            pltpu.VMEM((1, ROWS), jnp.int32),
            pltpu.VMEM((ROWS, QC), BF),
            pltpu.VMEM((ROWS, QC), BF),
            pltpu.VMEM((ROWS, D // 8), BF),
            pltpu.VMEM((1, 8, D), F32),
            pltpu.SemaphoreType.DMA((10,)),
            pltpu.VMEM((8, D), BF),
            pltpu.VMEM((8, D), BF),
            pltpu.VMEM((D, ROWS), BF),
            pltpu.VMEM((QC, ROWS), BF),
            pltpu.VMEM((2, HALF, ROWS), F32),
            pltpu.VMEM((2, HD, HD), F32),
            pltpu.VMEM((COLS, ROWS), F32),
            pltpu.VMEM((QC, ROWS), BF),
            pltpu.VMEM((QH_DEV, ROWS, HD), BF),
            pltpu.VMEM((SPAN + 1, 2, HD, ROWS), BF),
            pltpu.VMEM((SPAN + 1, 2, ROWS, HD), BF),
            pltpu.VMEM((QH_DEV, SPAN + 1, ROWS, ROWS), F32),
            pltpu.VMEM((QH_DEV, 1, ROWS), F32),
            pltpu.VMEM((QC, ROWS), F32),
            pltpu.VMEM((QC, ROWS), F32),
            pltpu.VMEM((SPAN + 1, 2, ROWS, HD), F32),
            pltpu.VMEM((SPAN + 1, ROWS, HD), BF),
            pltpu.VMEM((SPAN + 1, ROWS, HD), BF),
            pltpu.VMEM((SPAN, ROWS, HD), BF),
            pltpu.VMEM((SPAN, ROWS, HD), BF),
            pltpu.VMEM((QC, ROWS), BF),
            pltpu.VMEM((ROWS, QC), BF),
            pltpu.VMEM((8, ROWS, ROWS), F32),
            pltpu.VMEM((8, ROWS, ROWS), BF),
            pltpu.VMEM((N_LOW, ROWS, ROWS), BF),
            pltpu.VMEM((N_LOW - 1, ROWS, ROWS), BF),
            pltpu.VMEM((ROWS, ROWS), F32),
            pltpu.SemaphoreType.DMA((N_COPIES,)),
            pltpu.SemaphoreType.DMA((N_COPIES,)),
        ],
        compiler_params=pltpu.CompilerParams(
            collective_id=1, has_side_effects=True, vmem_limit_bytes=63 << 20
        ),
        cost_estimate=pl.CostEstimate(flops=4 * 10**9, bytes_accessed=4 << 20, transcendentals=10**6),
        name="masked_attention_layer",
    )(
        tokens,
        weights,
        query_gain.reshape(1, HD),
        key_gain.reshape(1, HD),
        frequency,
        first_row.reshape(1, ROWS),
        cotangent,
    )


def solution(mesh):
    in_specs = (P("dp", None), P("head", "dp", None), P(), P(), P("dp"), P("dp", "head"))
    out_specs = (P("dp", "head"), P("dp", "head"), P("head", "dp", None))
    return jax.shard_map(body, mesh=mesh, in_specs=in_specs, out_specs=out_specs, check_vma=False)
```
